32 devices in a mesh: groups: 2 (over y), tile: 4 (over z), chan: 2 (over x), sub: 2 (over core).
Axes of the slice: x: 2, y: 2, z: 4, core: 2. Of those that a mesh axis runs over, the one named last changes fastest.
Arguments:
- cycle_maps: bfloat16 [8, 3, 65536], P(('groups', 'chan', 'sub'), None, 'tile'), parts along dimension 0, may hold values from -6 to 6
- send_pick: int32 [98304], P('tile'), may hold values from 0 to 16384, as said below
- recv_pick: int32 [65536], P('tile'), may hold values from 0 to 24575, as said below
- neighbour: int32 [4, 4], replicated, may hold values from -1 to 3, as said below
- facing: int32 [4, 4], replicated, may hold values from 0 to 3, as said below
- conv_first: bfloat16 [9, 64, 3], replicated, may hold values from -1.25 to 1.25
- conv_second: bfloat16 [9, 64, 64], replicated, may hold values from -0.25 to 0.25
- cotangent: bfloat16 [8, 64, 65536], P(('groups', 'chan', 'sub'), None, 'tile'), parts along dimension 0, may hold values from -6 to 6
Outputs:
- output_maps: bfloat16 [8, 64, 65536], P(('groups', 'chan', 'sub'), None, 'tile'), parts along dimension 0
- grad_hidden: bfloat16 [8, 64, 65536], P(('groups', 'chan', 'sub'), None, 'tile'), parts along dimension 0
- grad_first: float32 [18, 64, 3], P('groups'), parts along dimension 0
- grad_second: float32 [18, 64, 64], P('groups'), parts along dimension 0
The draws below stay inside these ranges and needn't reach their ends.
There are 2 independent parts, one for each index of `groups`. The reference program is written for one: setup_inputs(seed, part) draws one part's arguments, and reference() takes and returns one part's arrays. A program takes and returns all parts, laid end to end along the dimension named above; an argument that names none is the same for every part. Nothing has to cross between parts.
Inputs may be any that keep to these rules, and one draw needn't show every extreme that they name: `send_pick`: entry ((i * 4) + d) * 6144 + s names the cycle pixel (0 to 16383, local to owner i) that owner i puts into slot s of its block for tile d, or 16384 for an empty slot; the used slots of each block are 0 to n - 1 with n at most 6144, and some block is full. Every cycle pixel is named exactly once. `recv_pick`: entry d * 16384 + q is i * 6144 + s: pixel q of tile d is carried in slot s of owner i's block for tile d, a used slot. With send_pick it maps cycle pixels one to one onto tile pixels; each tile receives from every owner. `neighbour`: the tiles form a band four tiles tall, closed east to west; each tile is turned by a multiple of a right angle. Row t lists the tile across sides north, east, south, west of tile t in its own orientation, -1 beyond the band's rim. Adjacency is mutual: if side k of t touches side j of p, side j of p touches side k of t. A tile meets one tile on at most 2 sides, and some tile on exactly that many. `facing`: the side of the neighbouring tile that touches side k of tile t; 0 where there is no neighbour.
All inputs are finite; a program needn't handle non-finite values.
Results may differ from the reference program's by a relative error of at most 0.005.
Values may be sent and summed in bfloat16 or wider, within the bound.
A program may use at most 192 MiB of HBM per device.

```python
import math
import jax
import jax.numpy as jnp
from jax import lax

SIDE = 128
CH = 64
CIN = 3
TILES = 4
CAP = 6144
BATCH = 4
NPIX = 65536
N_TILE = 4


def draw_order(order_key):
    return jax.random.permutation(order_key, SIDE * SIDE).astype(jnp.int32)


def regroup_tables(key):
    tile_count = N_TILE
    pixel_count = SIDE * SIDE
    pair_total = 2 * pixel_count // tile_count
    spread_half = pair_total // 4
    count_key, order_key = jax.random.split(jax.random.fold_in(key, 11))
    couples = tile_count // 4
    base = jax.random.randint(count_key, (couples, tile_count), pair_total // 2 - spread_half, pair_total // 2 + spread_half + 1).astype(jnp.int32)
    base = base.at[0, 0].set(pair_total // 2 + spread_half)
    paired = jnp.stack([base, pair_total - base], axis=1).reshape(2 * couples, tile_count)
    first_part = paired.T
    second_part = pair_total - jnp.roll(paired, -1, axis=1).T
    counts = jnp.stack([first_part, second_part], axis=2).reshape(tile_count, tile_count)
    sources = jnp.arange(tile_count, dtype=jnp.int32)
    shifts = (sources[None, :] - sources[:, None]) % tile_count
    by_dest = jnp.take_along_axis(counts, shifts, axis=1)
    starts = jnp.cumsum(counts, axis=1) - counts
    start_dest = jnp.take_along_axis(starts, shifts, axis=1)
    slot_ids = jnp.arange(CAP, dtype=jnp.int32)
    send_table = jnp.where(slot_ids[None, None, :] < by_dest[:, :, None], start_dest[:, :, None] + slot_ids[None, None, :], pixel_count)
    column_end = jnp.cumsum(by_dest, axis=0)
    column_start = column_end - by_dest
    positions = jnp.arange(pixel_count, dtype=jnp.int32)
    source_of = jnp.sum((positions[None, :, None] >= column_end.T[:, None, :]).astype(jnp.int32), axis=2)
    start_of = jnp.take_along_axis(column_start.T, source_of, axis=1)
    values = source_of * CAP + positions[None, :] - start_of
    orders = jax.vmap(draw_order)(jax.random.split(order_key, tile_count))
    recv_table = jnp.zeros((tile_count, pixel_count), jnp.int32).at[sources[:, None], orders].set(values.astype(jnp.int32))
    return (send_table.reshape(-1).astype(jnp.int32), recv_table.reshape(-1))


def face_tables(key):
    tile_count = N_TILE
    columns = tile_count // 4
    place_key, turn_key = jax.random.split(jax.random.fold_in(key, 23))
    place = jax.random.permutation(place_key, tile_count).astype(jnp.int32)
    turn = jax.random.randint(turn_key, (tile_count,), 0, 4).astype(jnp.int32)
    owner = jnp.zeros((tile_count,), jnp.int32).at[place].set(jnp.arange(tile_count, dtype=jnp.int32))
    grid_row = place // columns
    grid_col = place % columns
    row_step = jnp.array([-1, 0, 1, 0], jnp.int32)
    col_step = jnp.array([0, 1, 0, -1], jnp.int32)
    heading = (jnp.arange(4, dtype=jnp.int32)[None, :] + turn[:, None]) % 4
    next_row = grid_row[:, None] + row_step[heading]
    next_col = (grid_col[:, None] + col_step[heading]) % columns
    inside = (next_row >= 0) & (next_row < 4)
    partner = owner[jnp.clip(next_row, 0, 3) * columns + next_col]
    neighbour = jnp.where(inside, partner, -1).astype(jnp.int32)
    facing = jnp.where(inside, (heading + 2 - turn[partner]) % 4, 0).astype(jnp.int32)
    return (neighbour, facing)


def draw_send_pick(key, part):
    return regroup_tables(key)[0]


def draw_recv_pick(key, part):
    return regroup_tables(key)[1]


def draw_neighbour(key, part):
    return face_tables(key)[0]


def draw_facing(key, part):
    return face_tables(key)[1]


def block_scale(own_key, extent, pieces, least, largest):
    def one(dim, parts):
        draws = jax.random.uniform(jax.random.fold_in(jax.random.fold_in(own_key, 6), dim), (parts,), jnp.float32, least / len(pieces), largest / len(pieces))
        return jnp.repeat(jnp.exp(draws), extent[dim] // parts).reshape((-1,) + (1,) * (len(extent) - dim - 1))

    loudness = one(*pieces[0])
    for cut in pieces[1:]:
        loudness = loudness * one(*cut)
    return loudness


def bell_draw(key, dims, scale, bound, cuts=(), kind=jnp.bfloat16):
    factor_of = block_scale(key, dims, cuts, -0.22, 0.18) if cuts else 1.0
    values = jax.random.normal(key, dims, jnp.float32) * scale * factor_of
    return jnp.minimum(jnp.maximum(values, -bound), bound).astype(kind)


def setup_inputs(seed: int = 0, part: int = 0) -> dict:
    splits = jax.random.split(jax.random.key(seed), 9)
    own_keys = jax.random.split(jax.random.fold_in(splits[8], part), 9)
    cycle_maps = bell_draw(own_keys[0], (BATCH, CIN, NPIX), 1.0, 6.0, ((0, 4), (2, 4)))
    send_pick = draw_send_pick(jax.random.fold_in(splits[8], 71), part)
    recv_pick = draw_recv_pick(jax.random.fold_in(splits[8], 71), part)
    neighbour = draw_neighbour(jax.random.fold_in(splits[8], 71), part)
    facing = draw_facing(jax.random.fold_in(splits[8], 71), part)
    conv_first = bell_draw(splits[5], (9, CH, CIN), (9 * CIN) ** -0.5, 1.25)
    conv_second = bell_draw(splits[6], (9, CH, CH), (9 * CH) ** -0.5, 0.25)
    cotangent = bell_draw(own_keys[7], (BATCH, CH, NPIX), 1.0, 6.0, ((0, 4), (2, 4)))
    return dict(cycle_maps=cycle_maps, send_pick=send_pick, recv_pick=recv_pick, neighbour=neighbour, facing=facing, conv_first=conv_first, conv_second=conv_second, cotangent=cotangent)


def border(field):
    return jnp.stack([field[:, :, 0, :], field[:, :, :, -1], field[:, :, -1, :], field[:, :, :, 0]])

def frame_rim(frame):
    return jnp.stack([frame[:, :, 0, 1:-1], frame[:, :, 1:-1, -1], frame[:, :, -1, 1:-1], frame[:, :, 1:-1, 0]])

def outgoing(strips):
    return jnp.stack([strips[0], strips[1], strips[2][..., ::-1], strips[3][..., ::-1]])

def orient(strips):
    return jnp.stack([strips[0][..., ::-1], strips[1][..., ::-1], strips[2], strips[3]])

def route(strips, neighbour, facing):
    partner = jnp.maximum(neighbour, 0)
    arrived = strips[facing, partner]
    arrived = jnp.where((neighbour >= 0)[:, :, None, None], arrived, jnp.zeros((), strips.dtype))
    return orient(jnp.transpose(arrived, (1, 0, 2, 3)))

def with_rims(field, incoming):
    padded = jnp.pad(field, ((0, 0), (0, 0), (1, 1), (1, 1)))
    padded = padded.at[:, :, 0, 1:-1].set(incoming[0])
    padded = padded.at[:, :, 1:-1, -1].set(incoming[1])
    padded = padded.at[:, :, -1, 1:-1].set(incoming[2])
    padded = padded.at[:, :, 1:-1, 0].set(incoming[3])
    return padded

def convolve(padded, weights):
    total = None
    for position in range(9):
        row_shift, col_shift = divmod(position, 3)
        window = padded[:, :, row_shift:row_shift + SIDE, col_shift:col_shift + SIDE].astype(jnp.float32)
        term = jnp.einsum('oc,tcij->toij', weights[position], window)
        total = term if total is None else total + term
    return total

def weight_terms(padded, grad_out):
    terms = []
    for position in range(9):
        row_shift, col_shift = divmod(position, 3)
        window = padded[:, :, row_shift:row_shift + SIDE, col_shift:col_shift + SIDE].astype(jnp.float32)
        terms.append(jnp.einsum('toij,tcij->oc', grad_out, window))
    return jnp.stack(terms)

def spread(grad_out, weights):
    total = None
    for position in range(9):
        row_shift, col_shift = divmod(position, 3)
        term = jnp.einsum('oc,toij->tcij', weights[position], grad_out)
        term = jnp.pad(term, ((0, 0), (0, 0), (row_shift, 2 - row_shift), (col_shift, 2 - col_shift)))
        total = term if total is None else total + term
    return total

def add_rims(interior, incoming):
    interior = interior.at[:, :, 0, :].add(incoming[0])
    interior = interior.at[:, :, :, -1].add(incoming[1])
    interior = interior.at[:, :, -1, :].add(incoming[2])
    interior = interior.at[:, :, :, 0].add(incoming[3])
    return interior

def reference(cycle_maps, send_pick, recv_pick, neighbour, facing, conv_first, conv_second, cotangent):
    pixel_count = SIDE * SIDE
    tile_pixel = jnp.arange(NPIX, dtype=jnp.int32)
    dest_tile = tile_pixel // pixel_count
    source = recv_pick // CAP
    slot_index = recv_pick % CAP
    local = send_pick[source * (TILES * CAP) + dest_tile * CAP + slot_index]
    cycle_index = (source * pixel_count + local).astype(jnp.int32)
    first_f = conv_first.astype(jnp.float32)
    second_f = conv_second.astype(jnp.float32)
    scale = 1.0 / math.sqrt(BATCH * NPIX)

    def one_map(carry, inputs):
        cycle, grad_in = inputs
        tiles = jnp.transpose(cycle[:, cycle_index].reshape(CIN, TILES, SIDE, SIDE), (1, 0, 2, 3))
        padded_in = with_rims(tiles, route(outgoing(border(tiles)), neighbour, facing))
        pre = convolve(padded_in, first_f)
        hidden = jax.nn.silu(pre).astype(jnp.bfloat16)
        padded_hidden = with_rims(hidden, route(outgoing(border(hidden)), neighbour, facing))
        output = convolve(padded_hidden, second_f).astype(jnp.bfloat16)
        grad_out = jnp.transpose(grad_in.reshape(CH, TILES, SIDE, SIDE), (1, 0, 2, 3)).astype(jnp.float32)
        second_term = weight_terms(padded_hidden, grad_out)
        grad_frame = spread(grad_out, second_f)
        rim_grads = route(outgoing(frame_rim(grad_frame)).astype(jnp.bfloat16), neighbour, facing)
        hidden_grad = add_rims(grad_frame[:, :, 1:-1, 1:-1], rim_grads.astype(jnp.float32))
        sigma = jax.nn.sigmoid(pre)
        pre_grad = (hidden_grad * sigma * (1.0 + pre * (1.0 - sigma))).astype(jnp.bfloat16)
        first_term = weight_terms(padded_in, pre_grad.astype(jnp.float32))
        out_maps = jnp.transpose(output, (1, 0, 2, 3)).reshape(CH, NPIX)
        out_grad = jnp.transpose(hidden_grad.astype(jnp.bfloat16), (1, 0, 2, 3)).reshape(CH, NPIX)
        return ((carry[0] + first_term, carry[1] + second_term), (out_maps, out_grad))
    start = (jnp.zeros((9, CH, CIN), jnp.float32), jnp.zeros((9, CH, CH), jnp.float32))
    (first_sum, second_sum), (output_maps, grad_hidden) = lax.scan(one_map, start, (cycle_maps, cotangent))
    return (output_maps, grad_hidden, first_sum * scale, second_sum * scale)
```

```python
import functools
import math

import jax
import jax.numpy as jnp
from jax import lax
from jax.experimental import pallas as pl
from jax.experimental.pallas import tpu as pltpu
from jax.sharding import PartitionSpec as P

SIDE = 128
CH = 64
CIN = 3
PIX = SIDE * SIDE
ROWS = 16
STEP = ROWS * SIDE
STEPS = SIDE // ROWS
SEND_DEPTH = 256
SLOT_DEPTH = 384
MESH = pl.DeviceIdType.MESH
F32 = jnp.float32
BF16 = jnp.bfloat16
NT = (((1,), (1,)), ((), ()))


def dot(a, b):
    return jnp.dot(a, b, preferred_element_type=F32)


def dot_nt(a, b):
    return lax.dot_general(a, b, NT, preferred_element_type=F32)


def lanes(shape):
    return lax.broadcasted_iota(jnp.int32, shape, 1) % SIDE


def from_left(x):
    rows = x.shape[1] // SIDE
    out = jnp.concatenate(
        [pltpu.roll(x[:, r * SIDE : (r + 1) * SIDE], 1, 1) for r in range(rows)], axis=1
    )
    return jnp.where(lanes(x.shape) == 0, 0.0, out)


def from_right(x):
    rows = x.shape[1] // SIDE
    out = jnp.concatenate(
        [pltpu.roll(x[:, r * SIDE : (r + 1) * SIDE], SIDE - 1, 1) for r in range(rows)], axis=1
    )
    return jnp.where(lanes(x.shape) == SIDE - 1, 0.0, out)


def one_hot(depth, index):
    shape = (depth, index.shape[1])
    position = lax.broadcasted_iota(jnp.int32, shape, 0)
    return jnp.where(position == index, 1.0, 0.0).astype(BF16)


def kernel(
    tile_count,
    chan_count,
    sub_count,
    cap,
    scale,
    table_ref,
    send_ref,
    recv_ref,
    nbr_ref,
    face_ref,
    w_first_ref,
    w_fwd_ref,
    w_bwd_ref,
    w_west_ref,
    w_east_ref,
    cot_ref,
    out_ref,
    ghid_ref,
    gfirst_ref,
    gsecond_ref,
    edge,
    cc,
    hh,
    xx,
    tiles,
    slope,
    hgrad,
    grads,
    slots,
    block_out,
    block_in,
    strip_in,
    strip_hid,
    strip_rim,
    red_src,
    red_in,
    red_out,
    px_send,
    px_recv,
    in_send,
    in_recv,
    hid_send,
    hid_recv,
    rim_send,
    rim_recv,
    part_send,
    part_recv,
    sum_send,
    sum_recv,
):
    me = lax.axis_index("tile")
    group = tile_count * chan_count * sub_count
    flat = (me * chan_count + lax.axis_index("chan")) * sub_count + lax.axis_index("sub")
    groups_per_block = cap // SLOT_DEPTH
    block_rows = block_out.shape[1]

    def member(index):
        return {
            "tile": index // (chan_count * sub_count),
            "chan": (index // sub_count) % chan_count,
            "sub": index % sub_count,
        }

    barrier = pltpu.get_barrier_semaphore()

    def greet(k, carry):
        pl.semaphore_signal(
            barrier, inc=1, device_id=member((flat + k) % group), device_id_type=MESH
        )
        return carry

    lax.fori_loop(1, group, greet, 0)

    def tile_copy(src, dst, send_sem, recv_sem, peer, place):
        return pltpu.make_async_remote_copy(
            src_ref=src,
            dst_ref=dst.at[place],
            send_sem=send_sem.at[peer],
            recv_sem=recv_sem.at[place],
            device_id={"tile": peer},
            device_id_type=MESH,
        )

    def post(source, dst, send_sem, recv_sem):
        def go(k, carry):
            peer = (me + k) % tile_count
            tile_copy(source(peer), dst, send_sem, recv_sem, peer, me).start()
            return carry

        lax.fori_loop(1, tile_count, go, 0)

    def collect(source, dst, send_sem, recv_sem):
        def go(k, carry):
            peer = (me + k) % tile_count
            tile_copy(source(peer), dst, send_sem, recv_sem, peer, peer).wait_recv()
            return carry

        lax.fori_loop(1, tile_count, go, 0)

    def finish(source, dst, send_sem, recv_sem):
        def go(k, carry):
            peer = (me + k) % tile_count
            tile_copy(source(peer), dst, send_sem, recv_sem, peer, me).wait_send()
            return carry

        lax.fori_loop(1, tile_count, go, 0)

    px = (lambda peer: block_out.at[peer], block_in, px_send, px_recv)
    inp = (lambda peer: strip_in.at[me], strip_in, in_send, in_recv)
    hid = (lambda peer: strip_hid.at[me], strip_hid, hid_send, hid_recv)
    rim = (lambda peer: strip_rim.at[me], strip_rim, rim_send, rim_recv)

    flip = jnp.where(
        lax.broadcasted_iota(jnp.int32, (SIDE, SIDE), 0)
        + lax.broadcasted_iota(jnp.int32, (SIDE, SIDE), 1)
        == SIDE - 1,
        1.0,
        0.0,
    ).astype(BF16)

    def reverse(strip):
        return dot(strip.astype(BF16), flip)

    edge[...] = jnp.zeros_like(edge)
    row_of = lax.broadcasted_iota(jnp.int32, (ROWS, STEP), 0)
    cell_of = lax.broadcasted_iota(jnp.int32, (ROWS, STEP), 1)
    edge[SIDE : SIDE + ROWS, :] = jnp.where(cell_of == row_of * SIDE, 1.0, 0.0).astype(BF16)
    edge[3 * SIDE : 3 * SIDE + ROWS, :] = jnp.where(
        cell_of == row_of * SIDE + SIDE - 1, 1.0, 0.0
    ).astype(BF16)

    def west(step):
        return edge[pl.ds(pl.multiple_of(SIDE - ROWS * step, ROWS), SIDE), :]

    def east(step):
        return edge[pl.ds(pl.multiple_of(3 * SIDE - ROWS * step, ROWS), SIDE), :]

    def both(step):
        return jnp.concatenate([west(step), east(step)], axis=0)

    def cells(step, extra=0, rows=ROWS):
        return pl.ds(pl.multiple_of(step * STEP + extra * SIDE, SIDE), rows * SIDE)

    if block_rows != CIN * groups_per_block:
        slots[...] = jnp.zeros_like(slots)
    quads = groups_per_block // 4
    width = 4 * SLOT_DEPTH
    table_groups = PIX // SEND_DEPTH

    def fill(it, carry):
        pick = send_ref[0:1, pl.ds(pl.multiple_of(it * width, SIDE), width)]
        hot = one_hot(SEND_DEPTH, pick & (SEND_DEPTH - 1))
        found = dot(table_ref[...], hot)
        mask = lax.broadcasted_iota(jnp.int32, (table_groups, width), 0) == pick // SEND_DEPTH
        dest = it // quads
        first = (it % quads) * 4
        for c in range(CIN):
            part = found[c * table_groups : (c + 1) * table_groups]
            value = jnp.sum(jnp.where(mask, part, 0.0), axis=0, keepdims=True)
            for q in range(4):
                slots[dest, pl.ds(c * groups_per_block + first + q, 1), :] = value[
                    :, q * SLOT_DEPTH : (q + 1) * SLOT_DEPTH
                ]
        return carry

    lax.fori_loop(0, tile_count * quads, fill, 0)
    block_out[...] = slots[...].astype(BF16)
    block_in[me] = block_out[me]
    pl.semaphore_wait(barrier, group - 1)
    post(*px)

    cc[:, 0 : 2 * SIDE] = jnp.zeros((3 * CH, 2 * SIDE), BF16)
    cc[:, (SIDE + 2) * SIDE : (SIDE + 4) * SIDE] = jnp.zeros((3 * CH, 2 * SIDE), BF16)

    def shift_cotangent(step, columns):
        narrow = cot_ref[0, :, cells(step)]
        wide = narrow.astype(F32)
        at = cells(step, 2)
        cc[0:CH, at] = from_right(wide).astype(BF16)
        cc[CH : 2 * CH, at] = narrow
        cc[2 * CH : 3 * CH, at] = from_left(wide).astype(BF16)
        return columns + dot_nt(narrow, both(step))

    columns = lax.fori_loop(0, STEPS, shift_cotangent, jnp.zeros((CH, 2 * SIDE), F32))

    def along(column):
        return jnp.concatenate([from_right(column), column, from_left(column)], axis=0).astype(
            BF16
        )

    strip_rim[me, 0] = dot(w_bwd_ref[0:CH, :], cc[:, 2 * SIDE : 3 * SIDE]).astype(BF16)
    strip_rim[me, 1] = dot(w_east_ref[...], along(columns[:, SIDE:])).astype(BF16)
    south = dot(w_bwd_ref[2 * CH :, :], cc[:, (SIDE + 1) * SIDE : (SIDE + 2) * SIDE])
    strip_rim[me, 2] = reverse(south).astype(BF16)
    strip_rim[me, 3] = reverse(dot(w_west_ref[...], along(columns[:, :SIDE]))).astype(BF16)
    post(*rim)

    collect(*px)
    chunk = 1024

    def place(it, carry):
        at = pl.ds(pl.multiple_of(it * chunk, chunk), chunk)
        pick = recv_ref[0:1, at]
        key = ((pick // SIDE) * 171) // 512
        hot = one_hot(SLOT_DEPTH, pick - key * SLOT_DEPTH)
        table = block_in[...].reshape(tile_count * block_rows, SLOT_DEPTH)
        found = dot(table, hot)
        total = [jnp.zeros((groups_per_block, chunk), F32)] * CIN
        local = lax.broadcasted_iota(jnp.int32, (groups_per_block, chunk), 0)
        for owner in range(tile_count):
            mask = local + owner * groups_per_block == key
            for c in range(CIN):
                start = owner * block_rows + c * groups_per_block
                part = found[start : start + groups_per_block]
                total[c] = total[c] + jnp.where(mask, part, 0.0)
        row = lax.broadcasted_iota(jnp.int32, (8, chunk), 0)
        value = jnp.zeros((8, chunk), F32)
        for c in range(CIN):
            value = jnp.where(row == c, jnp.sum(total[c], axis=0, keepdims=True), value)
        tiles[:, at] = value
        return carry

    lax.fori_loop(0, PIX // chunk, place, 0)

    def tall(x):
        return jnp.concatenate([x, jnp.zeros_like(x)], axis=0)

    def tile_columns(step, total):
        return total + dot_nt(tall(tiles[:, cells(step)]).astype(BF16), both(step))

    columns = lax.fori_loop(0, STEPS, tile_columns, jnp.zeros((16, 2 * SIDE), F32))
    strip_in[me, 0] = tall(tiles[:, 0:SIDE]).astype(BF16)
    strip_in[me, 1] = columns[:, SIDE:].astype(BF16)
    strip_in[me, 2] = reverse(tall(tiles[:, PIX - SIDE : PIX])).astype(BF16)
    strip_in[me, 3] = reverse(columns[:, :SIDE]).astype(BF16)
    post(*inp)

    def interior(step, carry):
        term = dot(w_bwd_ref[...], cc[:, cells(step, 1, ROWS + 2)])
        hgrad[:, cells(step)] = (
            term[0:CH, 2 * SIDE :]
            + term[CH : 2 * CH, SIDE : SIDE + STEP]
            + term[2 * CH :, 0:STEP]
        )
        return carry

    lax.fori_loop(0, STEPS, interior, 0)

    def incoming(buffer):
        strips = []
        for k in range(4):
            near = nbr_ref[me, k]
            there = jnp.where(near >= 0, 1.0, 0.0)
            strip = buffer[jnp.maximum(near, 0), face_ref[me, k]].astype(F32) * there
            strips.append(reverse(strip) if k < 2 else strip)
        return strips

    collect(*inp)
    north, right, bottom, left = incoming(strip_in)

    def three(x, edges):
        mid = x[0:8]
        a = from_left(mid)
        b = from_right(mid)
        if edges is not None:
            a = jnp.where(lanes(a.shape) == 0, edges[0:8], a)
            b = jnp.where(lanes(b.shape) == SIDE - 1, edges[0:8], b)
        return jnp.concatenate([a + pltpu.roll(mid, 4, 0), b], axis=0).astype(BF16)

    xx[:, 0:SIDE] = three(north, None)
    xx[:, (SIDE + 1) * SIDE :] = three(bottom, None)
    sides_in = jnp.concatenate([left, right], axis=1).astype(BF16)

    def input_copies(step, carry):
        xx[:, cells(step, 1)] = three(tiles[:, cells(step)], dot(sides_in, both(step)))
        return carry

    lax.fori_loop(0, STEPS, input_copies, 0)

    def input_stack(step):
        part = xx[:, cells(step, 0, ROWS + 2)]
        return [part[:, a * SIDE : a * SIDE + STEP] for a in range(3)]

    def forward_first(step, columns):
        pre = dot(w_first_ref[...], jnp.concatenate(input_stack(step), axis=0))
        sigma = jax.nn.sigmoid(pre)
        value = pre * sigma
        slope[:, cells(step)] = sigma * (1.0 + pre * (1.0 - sigma))
        narrow = value.astype(BF16)
        at = cells(step, 1)
        hh[0:CH, at] = from_left(value).astype(BF16)
        hh[CH : 2 * CH, at] = narrow
        hh[2 * CH : 3 * CH, at] = from_right(value).astype(BF16)
        return columns + dot_nt(narrow, both(step))

    columns = lax.fori_loop(0, STEPS, forward_first, jnp.zeros((CH, 2 * SIDE), F32))
    strip_hid[me, 0] = hh[CH : 2 * CH, SIDE : 2 * SIDE]
    strip_hid[me, 1] = columns[:, SIDE:].astype(BF16)
    strip_hid[me, 2] = reverse(hh[CH : 2 * CH, PIX : PIX + SIDE]).astype(BF16)
    strip_hid[me, 3] = reverse(columns[:, :SIDE]).astype(BF16)
    post(*hid)

    collect(*rim)
    north, right, bottom, left = incoming(strip_rim)
    hgrad[:, 0:SIDE] = hgrad[:, 0:SIDE] + north
    hgrad[:, PIX - SIDE : PIX] = hgrad[:, PIX - SIDE : PIX] + bottom
    sides_rim = jnp.concatenate([left, right], axis=1).astype(BF16)
    grads[...] = jnp.zeros_like(grads)

    def backward_first(step, carry):
        total = hgrad[:, cells(step)] + dot(sides_rim, both(step))
        ghid_ref[0, :, cells(step)] = total.astype(BF16)
        pre_grad = (total * slope[:, cells(step)]).astype(BF16)
        stack = jnp.concatenate(
            [jnp.zeros((64, STEP), BF16)] + input_stack(step) + [jnp.zeros((16, STEP), BF16)],
            axis=0,
        )
        grads[0:CH, SIDE : 2 * SIDE] = grads[0:CH, SIDE : 2 * SIDE] + dot_nt(pre_grad, stack)
        return carry

    lax.fori_loop(0, STEPS, backward_first, 0)

    collect(*hid)
    north, right, bottom, left = incoming(strip_hid)

    def halo_row(strip):
        return jnp.concatenate([from_left(strip), strip, from_right(strip)], axis=0).astype(BF16)

    hh[:, 0:SIDE] = halo_row(north)
    hh[:, (SIDE + 1) * SIDE :] = halo_row(bottom)
    left = left.astype(BF16)
    right = right.astype(BF16)
    grads[0:CH, 0 : 3 * CH] = grads[0:CH, 0 : 3 * CH] + dot_nt(
        cc[CH : 2 * CH, 2 * SIDE : 3 * SIDE], hh[:, 0:SIDE]
    )
    grads[2 * CH :, 0 : 3 * CH] = grads[2 * CH :, 0 : 3 * CH] + dot_nt(
        cc[CH : 2 * CH, (SIDE + 1) * SIDE : (SIDE + 2) * SIDE], hh[:, (SIDE + 1) * SIDE :]
    )

    def backward_second(step, carry):
        at = cells(step, 1)
        hh[0:CH, at] = (hh[0:CH, at].astype(F32) + dot(left, west(step))).astype(BF16)
        hh[2 * CH :, at] = (hh[2 * CH :, at].astype(F32) + dot(right, east(step))).astype(BF16)
        part = cc[CH : 2 * CH, cells(step, 1, ROWS + 2)]
        rows = jnp.concatenate(
            [part[:, 2 * SIDE :], part[:, SIDE : SIDE + STEP], part[:, 0:STEP]], axis=0
        )
        grads[:, 0 : 3 * CH] = grads[:, 0 : 3 * CH] + dot_nt(rows, hh[:, at])
        return carry

    lax.fori_loop(0, STEPS, backward_second, 0)

    share = red_src.shape[1]
    pieces = 3 * CH // share
    for half in range(2):
        for k in range(pieces):
            red_src[half * pieces + k] = grads[
                k * share : (k + 1) * share, half * SIDE : (half + 1) * SIDE
            ]
    for k in range(2 * pieces, group):
        red_src[k] = jnp.zeros((share, SIDE), F32)

    def part_copy(peer, place):
        return pltpu.make_async_remote_copy(
            src_ref=red_src.at[peer],
            dst_ref=red_in.at[place],
            send_sem=part_send.at[peer],
            recv_sem=part_recv.at[place],
            device_id=member(peer),
            device_id_type=MESH,
        )

    def sum_copy(peer, place):
        return pltpu.make_async_remote_copy(
            src_ref=red_out.at[place],
            dst_ref=red_out.at[place],
            send_sem=sum_send.at[peer],
            recv_sem=sum_recv.at[place],
            device_id=member(peer),
            device_id_type=MESH,
        )

    def each_member(act):
        def go(k, carry):
            act((flat + k) % group)
            return carry

        lax.fori_loop(1, group, go, 0)

    red_in[flat] = red_src[flat]
    each_member(lambda peer: part_copy(peer, flat).start())

    def forward_second(step, carry):
        term = dot(w_fwd_ref[...], hh[:, cells(step, 0, ROWS + 2)])
        out_ref[0, :, cells(step)] = (
            term[0:CH, 0:STEP]
            + term[CH : 2 * CH, SIDE : SIDE + STEP]
            + term[2 * CH :, 2 * SIDE :]
        ).astype(BF16)
        return carry

    lax.fori_loop(0, STEPS // 2, forward_second, 0)
    each_member(lambda peer: part_copy(peer, peer).wait_recv())
    total = lax.fori_loop(
        0, group, lambda k, acc: acc + red_in[k], jnp.zeros((share, SIDE), F32)
    )
    red_out[flat] = total * scale
    each_member(lambda peer: sum_copy(peer, flat).start())
    lax.fori_loop(STEPS // 2, STEPS, forward_second, 0)
    each_member(lambda peer: sum_copy(peer, peer).wait_recv())

    halves = [
        jnp.concatenate([red_out[half * pieces + k] for k in range(pieces)], axis=0)
        for half in range(2)
    ]
    for a in range(3):
        rows = slice(a * CH, (a + 1) * CH)
        gsecond_ref[3 * a] = halves[0][rows, 0:CH]
        gsecond_ref[3 * a + 1] = halves[0][rows, CH : 2 * CH]
        gsecond_ref[3 * a + 2] = halves[1][rows, 0:CH]
        for b in range(3):
            lane = 64 + a * 16 + b * 4
            gfirst_ref[3 * a + b] = halves[1][0:CH, lane : lane + CIN]

    for part in (px, rim, inp, hid):
        finish(*part)
    each_member(lambda peer: part_copy(peer, flat).wait_send())
    each_member(lambda peer: sum_copy(peer, flat).wait_send())


def body(cycle_maps, send_pick, recv_pick, neighbour, facing, conv_first, conv_second, cotangent):
    tile_count = lax.axis_size("tile")
    chan_count = lax.axis_size("chan")
    sub_count = lax.axis_size("sub")
    group = tile_count * chan_count * sub_count
    cap = send_pick.shape[0] // tile_count
    scale = 1.0 / math.sqrt(group * PIX)
    table = cycle_maps.reshape(CIN * PIX // SEND_DEPTH, SEND_DEPTH)
    first = conv_first.reshape(3, 3, CH, CIN)
    first = jnp.pad(first, ((0, 0), (0, 0), (0, 0), (0, 1)))
    first = jnp.pad(first.transpose(2, 0, 1, 3).reshape(CH, 3, 12), ((0, 0), (0, 0), (0, 4)))
    first = first.reshape(CH, 48)
    second = conv_second.reshape(3, 3, CH, CH)
    w_fwd = second.transpose(0, 2, 1, 3).reshape(3 * CH, 3 * CH)
    w_bwd = second.transpose(0, 3, 1, 2).reshape(3 * CH, 3 * CH)
    w_west = second[:, 0].transpose(2, 0, 1).reshape(CH, 3 * CH)
    w_east = second[:, 2].transpose(2, 0, 1).reshape(CH, 3 * CH)
    per_block = cap // SLOT_DEPTH
    block_rows = -(-CIN * per_block // 16) * 16
    share = 8 * -(-2 * 3 * CH // (8 * group))
    vmem = pl.BlockSpec(memory_space=pltpu.VMEM)
    smem = pl.BlockSpec(memory_space=pltpu.SMEM)
    dma = pltpu.SemaphoreType.DMA
    return pl.pallas_call(
        functools.partial(kernel, tile_count, chan_count, sub_count, cap, scale),
        out_shape=(
            jax.ShapeDtypeStruct((1, CH, PIX), BF16),
            jax.ShapeDtypeStruct((1, CH, PIX), BF16),
            jax.ShapeDtypeStruct((9, CH, CIN), F32),
            jax.ShapeDtypeStruct((9, CH, CH), F32),
        ),
        in_specs=[vmem, vmem, vmem, smem, smem] + [vmem] * 6,
        out_specs=(vmem, vmem, vmem, vmem),
        scratch_shapes=[
            pltpu.VMEM((4 * SIDE, STEP), BF16),
            pltpu.VMEM((3 * CH, (SIDE + 4) * SIDE), BF16),
            pltpu.VMEM((3 * CH, (SIDE + 2) * SIDE), BF16),
            pltpu.VMEM((16, (SIDE + 2) * SIDE), BF16),
            pltpu.VMEM((8, PIX), F32),
            pltpu.VMEM((CH, PIX), F32),
            pltpu.VMEM((CH, PIX), F32),
            pltpu.VMEM((3 * CH, 2 * SIDE), F32),
            pltpu.VMEM((tile_count, block_rows, SLOT_DEPTH), F32),
            pltpu.VMEM((tile_count, block_rows, SLOT_DEPTH), BF16),
            pltpu.VMEM((tile_count, block_rows, SLOT_DEPTH), BF16),
            pltpu.VMEM((tile_count, 4, 16, SIDE), BF16),
            pltpu.VMEM((tile_count, 4, CH, SIDE), BF16),
            pltpu.VMEM((tile_count, 4, CH, SIDE), BF16),
            pltpu.VMEM((group, share, SIDE), F32),
            pltpu.VMEM((group, share, SIDE), F32),
            pltpu.VMEM((group, share, SIDE), F32),
        ]
        + [dma((tile_count,))] * 8
        + [dma((group,))] * 4,
        compiler_params=pltpu.CompilerParams(
            collective_id=0, has_side_effects=True, vmem_limit_bytes=56 * 1024 * 1024
        ),
        cost_estimate=pl.CostEstimate(
            flops=6_000_000_000, bytes_accessed=8_000_000, transcendentals=1_000_000
        ),
    )(
        table,
        send_pick.reshape(1, -1),
        recv_pick.reshape(1, -1),
        neighbour,
        facing,
        first,
        w_fwd,
        w_bwd,
        w_west,
        w_east,
        cotangent,
    )


def solution(mesh):
    in_specs = (
        P(("groups", "chan", "sub"), None, "tile"),
        P("tile"),
        P("tile"),
        P(),
        P(),
        P(),
        P(),
        P(("groups", "chan", "sub"), None, "tile"),
    )
    out_specs = (
        P(("groups", "chan", "sub"), None, "tile"),
        P(("groups", "chan", "sub"), None, "tile"),
        P("groups", None, None),
        P("groups", None, None),
    )
    return jax.shard_map(body, mesh=mesh, in_specs=in_specs, out_specs=out_specs, check_vma=False)
```

```python
import functools
import math

import jax
import jax.numpy as jnp
from jax import lax
from jax.experimental import pallas as pl
from jax.experimental.pallas import tpu as pltpu
from jax.sharding import PartitionSpec as P

SIDE = 128
CH = 64
CIN = 3
PIX = SIDE * SIDE
ROWS = 16
STEP = ROWS * SIDE
STEPS = SIDE // ROWS
SEND_DEPTH = 256
SLOT_DEPTH = 384
MESH = pl.DeviceIdType.MESH
F32 = jnp.float32
BF16 = jnp.bfloat16
NT = (((1,), (1,)), ((), ()))
TN = (((0,), (0,)), ((), ()))


def dot(a, b):
    return jnp.dot(a, b, preferred_element_type=F32)


def dot_nt(a, b):
    return lax.dot_general(a, b, NT, preferred_element_type=F32)


def dot_tn(a, b):
    return lax.dot_general(a, b, TN, preferred_element_type=F32)


def lanes(shape):
    return lax.broadcasted_iota(jnp.int32, shape, 1) % SIDE


def from_left(x):
    rows = x.shape[1] // SIDE
    out = jnp.concatenate(
        [pltpu.roll(x[:, r * SIDE : (r + 1) * SIDE], 1, 1) for r in range(rows)], axis=1
    )
    return jnp.where(lanes(x.shape) == 0, 0.0, out)


def from_right(x):
    rows = x.shape[1] // SIDE
    out = jnp.concatenate(
        [pltpu.roll(x[:, r * SIDE : (r + 1) * SIDE], SIDE - 1, 1) for r in range(rows)], axis=1
    )
    return jnp.where(lanes(x.shape) == SIDE - 1, 0.0, out)


def one_hot(depth, index):
    shape = (depth, index.shape[1])
    position = lax.broadcasted_iota(jnp.int16, shape, 0)
    hit = position == index.astype(jnp.int16)
    return jnp.where(hit, jnp.ones(shape, BF16), jnp.zeros(shape, BF16))


def kernel(
    tile_count,
    chan_count,
    sub_count,
    cap,
    scale,
    cycle_ref,
    send_ref,
    recv_ref,
    nbr_ref,
    face_ref,
    first_ref,
    second_ref,
    cot_hbm,
    out_ref,
    ghid_ref,
    gfirst_ref,
    gsecond_ref,
    w_first_ref,
    w_fwd_ref,
    w_bwd_ref,
    weights,
    table_wide,
    table_ref,
    cot_ref,
    out_vmem,
    ghid_vmem,
    edge,
    cc,
    hh,
    xx,
    tiles,
    slope,
    hgrad,
    grads,
    slots,
    block_out,
    block_in,
    strip_in,
    strip_hid,
    strip_rim,
    red_src,
    red_in,
    red_out,
    px_send,
    px_recv,
    in_send,
    in_recv,
    hid_send,
    hid_recv,
    rim_send,
    rim_recv,
    part_send,
    part_recv,
    sum_send,
    sum_recv,
    cot_sem,
    out_sem,
    ghid_sem,
):
    me = lax.axis_index("tile")
    group = tile_count * chan_count * sub_count
    flat = (me * chan_count + lax.axis_index("chan")) * sub_count + lax.axis_index("sub")
    groups_per_block = cap // SLOT_DEPTH
    block_rows = block_out.shape[1]

    def member(index):
        return {
            "tile": index // (chan_count * sub_count),
            "chan": (index // sub_count) % chan_count,
            "sub": index % sub_count,
        }

    barrier = pltpu.get_barrier_semaphore()

    def greet(k, carry):
        pl.semaphore_signal(
            barrier, inc=1, device_id=member((flat + k) % group), device_id_type=MESH
        )
        return carry

    lax.fori_loop(1, group, greet, 0)
    cot_copy = pltpu.make_async_copy(cot_hbm.at[0], cot_ref, cot_sem)
    cot_copy.start()

    for a in range(3):
        for b in range(3):
            weights[a * CH : (a + 1) * CH, b * CH : (b + 1) * CH] = second_ref[
                3 * a + b
            ].astype(F32)
    w_fwd_ref[...] = weights[0 : 3 * CH, 0 : 3 * CH].astype(BF16)
    weights[...] = jnp.zeros_like(weights)
    for a in range(3):
        for b in range(3):
            weights[b * CH : (b + 1) * CH, a * CH : (a + 1) * CH] = second_ref[
                3 * a + b
            ].astype(F32)
    w_bwd_ref[...] = weights[...].T[0 : 3 * CH, 0 : 3 * CH].astype(BF16)
    weights[0:SIDE, 0:SIDE] = jnp.zeros((SIDE, SIDE), F32)
    for a in range(3):
        for b in range(3):
            at = a * 16 + b * 4
            weights[at : at + CIN, 0:CH] = first_ref[3 * a + b].astype(F32)
    w_first_ref[...] = weights[0:SIDE, 0:SIDE].T[0:CH, 0:48].astype(BF16)
    for g in range(PIX // SEND_DEPTH):
        piece = cycle_ref[0, :, g * SEND_DEPTH : (g + 1) * SEND_DEPTH].astype(F32)
        for c in range(CIN):
            row = c * (PIX // SEND_DEPTH) + g
            table_wide[row : row + 1, :] = piece[c : c + 1]
    table_ref[...] = table_wide[...].astype(BF16)

    def tile_copy(src, dst, send_sem, recv_sem, peer, place):
        return pltpu.make_async_remote_copy(
            src_ref=src,
            dst_ref=dst.at[place],
            send_sem=send_sem.at[peer],
            recv_sem=recv_sem.at[place],
            device_id={"tile": peer},
            device_id_type=MESH,
        )

    def post(source, dst, send_sem, recv_sem):
        def go(k, carry):
            peer = (me + k) % tile_count
            tile_copy(source(peer), dst, send_sem, recv_sem, peer, me).start()
            return carry

        lax.fori_loop(1, tile_count, go, 0)

    def collect(source, dst, send_sem, recv_sem):
        def go(k, carry):
            peer = (me + k) % tile_count
            tile_copy(source(peer), dst, send_sem, recv_sem, peer, peer).wait_recv()
            return carry

        lax.fori_loop(1, tile_count, go, 0)

    def finish(source, dst, send_sem, recv_sem):
        def go(k, carry):
            peer = (me + k) % tile_count
            tile_copy(source(peer), dst, send_sem, recv_sem, peer, me).wait_send()
            return carry

        lax.fori_loop(1, tile_count, go, 0)

    px = (lambda peer: block_out.at[peer], block_in, px_send, px_recv)
    inp = (lambda peer: strip_in.at[me], strip_in, in_send, in_recv)
    hid = (lambda peer: strip_hid.at[me], strip_hid, hid_send, hid_recv)
    rim = (lambda peer: strip_rim.at[me], strip_rim, rim_send, rim_recv)

    flip = jnp.where(
        lax.broadcasted_iota(jnp.int32, (SIDE, SIDE), 0)
        + lax.broadcasted_iota(jnp.int32, (SIDE, SIDE), 1)
        == SIDE - 1,
        1.0,
        0.0,
    ).astype(BF16)

    def reverse(strip):
        return dot(strip.astype(BF16), flip)

    edge[...] = jnp.zeros_like(edge)
    row_of = lax.broadcasted_iota(jnp.int32, (ROWS, STEP), 0)
    cell_of = lax.broadcasted_iota(jnp.int32, (ROWS, STEP), 1)
    edge[SIDE : SIDE + ROWS, :] = jnp.where(cell_of == row_of * SIDE, 1.0, 0.0).astype(BF16)
    edge[3 * SIDE : 3 * SIDE + ROWS, :] = jnp.where(
        cell_of == row_of * SIDE + SIDE - 1, 1.0, 0.0
    ).astype(BF16)

    def west(step):
        return edge[pl.ds(pl.multiple_of(SIDE - ROWS * step, ROWS), SIDE), :]

    def east(step):
        return edge[pl.ds(pl.multiple_of(3 * SIDE - ROWS * step, ROWS), SIDE), :]

    def both(step):
        return jnp.concatenate([west(step), east(step)], axis=0)

    def cells(step, extra=0, rows=ROWS):
        return pl.ds(pl.multiple_of(step * STEP + extra * SIDE, SIDE), rows * SIDE)

    if block_rows != CIN * groups_per_block:
        slots[...] = jnp.zeros_like(slots)
    quads = groups_per_block // 4
    width = 4 * SLOT_DEPTH
    table_groups = PIX // SEND_DEPTH

    def fill(it, carry):
        pick = send_ref[0:1, pl.ds(pl.multiple_of(it * width, SIDE), width)]
        hot = one_hot(SEND_DEPTH, pick & (SEND_DEPTH - 1))
        found = dot(table_ref[...], hot)
        mask = lax.broadcasted_iota(jnp.int32, (table_groups, width), 0) == pick // SEND_DEPTH
        dest = it // quads
        first = (it % quads) * 4
        for c in range(CIN):
            part = found[c * table_groups : (c + 1) * table_groups]
            value = jnp.sum(jnp.where(mask, part, 0.0), axis=0, keepdims=True)
            for q in range(4):
                slots[dest, pl.ds(c * groups_per_block + first + q, 1), :] = value[
                    :, q * SLOT_DEPTH : (q + 1) * SLOT_DEPTH
                ]
        return carry

    lax.fori_loop(0, tile_count * quads, fill, 0)
    block_out[...] = slots[...].astype(BF16)
    block_in[me] = block_out[me]
    pl.semaphore_wait(barrier, group - 1)
    post(*px)

    cc[:, 0 : 2 * SIDE] = jnp.zeros((3 * CH, 2 * SIDE), BF16)
    cc[:, (SIDE + 2) * SIDE : (SIDE + 4) * SIDE] = jnp.zeros((3 * CH, 2 * SIDE), BF16)

    cot_copy.wait()

    def shift_cotangent(step, columns):
        narrow = cot_ref[:, cells(step)]
        wide = narrow.astype(F32)
        at = cells(step, 2)
        cc[0:CH, at] = from_right(wide).astype(BF16)
        cc[CH : 2 * CH, at] = narrow
        cc[2 * CH : 3 * CH, at] = from_left(wide).astype(BF16)
        return columns + dot_nt(narrow, both(step))

    cot_columns = lax.fori_loop(0, STEPS, shift_cotangent, jnp.zeros((CH, 2 * SIDE), F32))

    def interior(step, carry):
        term = dot(w_bwd_ref[...], cc[:, cells(step, 1, ROWS + 2)])
        hgrad[:, cells(step)] = (
            term[0:CH, 2 * SIDE :]
            + term[CH : 2 * CH, SIDE : SIDE + STEP]
            + term[2 * CH :, 0:STEP]
        )
        return carry

    lax.fori_loop(0, STEPS // 2, interior, 0)

    collect(*px)
    chunk = 1024

    def place(it, carry):
        at = pl.ds(pl.multiple_of(it * chunk, chunk), chunk)
        pick = recv_ref[0:1, at]
        key = ((pick // SIDE) * 171) // 512
        hot = one_hot(SLOT_DEPTH, pick - key * SLOT_DEPTH)
        table = block_in[...].reshape(tile_count * block_rows, SLOT_DEPTH)
        found = dot(table, hot)
        total = [jnp.zeros((groups_per_block, chunk), F32)] * CIN
        local = lax.broadcasted_iota(jnp.int32, (groups_per_block, chunk), 0)
        for owner in range(tile_count):
            mask = local + owner * groups_per_block == key
            for c in range(CIN):
                start = owner * block_rows + c * groups_per_block
                part = found[start : start + groups_per_block]
                total[c] = total[c] + jnp.where(mask, part, 0.0)
        row = lax.broadcasted_iota(jnp.int32, (8, chunk), 0)
        value = jnp.zeros((8, chunk), F32)
        for c in range(CIN):
            value = jnp.where(row == c, jnp.sum(total[c], axis=0, keepdims=True), value)
        tiles[:, at] = value
        return carry

    lax.fori_loop(0, PIX // chunk, place, 0)

    def tall(x):
        return jnp.concatenate([x, jnp.zeros_like(x)], axis=0)

    def tile_columns(step, total):
        return total + dot_nt(tall(tiles[:, cells(step)]).astype(BF16), both(step))

    columns = lax.fori_loop(0, STEPS, tile_columns, jnp.zeros((16, 2 * SIDE), F32))
    strip_in[me, 0] = tall(tiles[:, 0:SIDE]).astype(BF16)
    strip_in[me, 1] = columns[:, SIDE:].astype(BF16)
    strip_in[me, 2] = reverse(tall(tiles[:, PIX - SIDE : PIX])).astype(BF16)
    strip_in[me, 3] = reverse(columns[:, :SIDE]).astype(BF16)
    post(*inp)

    def along(column):
        return jnp.concatenate([from_right(column), column, from_left(column)], axis=0).astype(
            BF16
        )

    def outer(b):
        return jnp.concatenate([second_ref[3 * a + b] for a in range(3)], axis=0)

    strip_rim[me, 0] = dot(w_bwd_ref[0:CH, :], cc[:, 2 * SIDE : 3 * SIDE]).astype(BF16)
    strip_rim[me, 1] = dot_tn(outer(2), along(cot_columns[:, SIDE:])).astype(BF16)
    south = dot(w_bwd_ref[2 * CH :, :], cc[:, (SIDE + 1) * SIDE : (SIDE + 2) * SIDE])
    strip_rim[me, 2] = reverse(south).astype(BF16)
    strip_rim[me, 3] = reverse(dot_tn(outer(0), along(cot_columns[:, :SIDE]))).astype(BF16)
    post(*rim)

    lax.fori_loop(STEPS // 2, STEPS, interior, 0)

    def incoming(buffer):
        strips = []
        for k in range(4):
            near = nbr_ref[me, k]
            there = jnp.where(near >= 0, 1.0, 0.0)
            strip = buffer[jnp.maximum(near, 0), face_ref[me, k]].astype(F32) * there
            strips.append(reverse(strip) if k < 2 else strip)
        return strips

    collect(*inp)
    north, right, bottom, left = incoming(strip_in)

    def three(x, edges):
        mid = x[0:8]
        a = from_left(mid)
        b = from_right(mid)
        if edges is not None:
            a = jnp.where(lanes(a.shape) == 0, edges[0:8], a)
            b = jnp.where(lanes(b.shape) == SIDE - 1, edges[0:8], b)
        return jnp.concatenate([a + pltpu.roll(mid, 4, 0), b], axis=0).astype(BF16)

    xx[:, 0:SIDE] = three(north, None)
    xx[:, (SIDE + 1) * SIDE :] = three(bottom, None)
    sides_in = jnp.concatenate([left, right], axis=1).astype(BF16)

    def input_copies(step, carry):
        xx[:, cells(step, 1)] = three(tiles[:, cells(step)], dot(sides_in, both(step)))
        return carry

    lax.fori_loop(0, STEPS, input_copies, 0)

    def input_stack(step):
        part = xx[:, cells(step, 0, ROWS + 2)]
        return [part[:, a * SIDE : a * SIDE + STEP] for a in range(3)]

    def forward_first(step, columns):
        pre = dot(w_first_ref[...], jnp.concatenate(input_stack(step), axis=0))
        sigma = jax.nn.sigmoid(pre)
        value = pre * sigma
        slope[:, cells(step)] = sigma * (1.0 + pre * (1.0 - sigma))
        narrow = value.astype(BF16)
        at = cells(step, 1)
        hh[0:CH, at] = from_left(value).astype(BF16)
        hh[CH : 2 * CH, at] = narrow
        hh[2 * CH : 3 * CH, at] = from_right(value).astype(BF16)
        return columns + dot_nt(narrow, both(step))

    columns = lax.fori_loop(0, STEPS, forward_first, jnp.zeros((CH, 2 * SIDE), F32))
    strip_hid[me, 0] = hh[CH : 2 * CH, SIDE : 2 * SIDE]
    strip_hid[me, 1] = columns[:, SIDE:].astype(BF16)
    strip_hid[me, 2] = reverse(hh[CH : 2 * CH, PIX : PIX + SIDE]).astype(BF16)
    strip_hid[me, 3] = reverse(columns[:, :SIDE]).astype(BF16)
    post(*hid)

    collect(*rim)
    north, right, bottom, left = incoming(strip_rim)
    hgrad[:, 0:SIDE] = hgrad[:, 0:SIDE] + north
    hgrad[:, PIX - SIDE : PIX] = hgrad[:, PIX - SIDE : PIX] + bottom
    sides_rim = jnp.concatenate([left, right], axis=1).astype(BF16)
    grads[...] = jnp.zeros_like(grads)

    def ghid_copy(step):
        at = cells(step)
        return pltpu.make_async_copy(ghid_vmem.at[:, at], ghid_ref.at[0, :, at], ghid_sem.at[step])

    def out_copy(step):
        at = cells(step)
        return pltpu.make_async_copy(out_vmem.at[:, at], out_ref.at[0, :, at], out_sem.at[step])

    def backward_first(step, carry):
        total = hgrad[:, cells(step)] + dot(sides_rim, both(step))
        ghid_vmem[:, cells(step)] = total.astype(BF16)
        ghid_copy(step).start()
        pre_grad = (total * slope[:, cells(step)]).astype(BF16)
        stack = jnp.concatenate(
            [jnp.zeros((64, STEP), BF16)] + input_stack(step) + [jnp.zeros((16, STEP), BF16)],
            axis=0,
        )
        grads[0:CH, SIDE : 2 * SIDE] = grads[0:CH, SIDE : 2 * SIDE] + dot_nt(pre_grad, stack)
        return carry

    lax.fori_loop(0, STEPS, backward_first, 0)

    def backward_second(step, carry):
        part = cc[CH : 2 * CH, cells(step, 1, ROWS + 2)]
        rows = jnp.concatenate(
            [part[:, 2 * SIDE :], part[:, SIDE : SIDE + STEP], part[:, 0:STEP]], axis=0
        )
        grads[:, 0 : 3 * CH] = grads[:, 0 : 3 * CH] + dot_nt(rows, hh[:, cells(step, 1)])
        return carry

    lax.fori_loop(0, STEPS, backward_second, 0)
    collect(*hid)
    north, right, bottom, left = incoming(strip_hid)

    def halo_row(strip):
        return jnp.concatenate([from_left(strip), strip, from_right(strip)], axis=0).astype(BF16)

    hh[:, 0:SIDE] = halo_row(north)
    hh[:, (SIDE + 1) * SIDE :] = halo_row(bottom)
    left = left.astype(BF16)
    right = right.astype(BF16)
    rest = jnp.zeros((CH, SIDE), BF16)
    grads[:, 0 : 3 * CH] = grads[:, 0 : 3 * CH] + dot_nt(
        along(cot_columns[:, :SIDE]), jnp.concatenate([left, rest, rest], axis=0)
    ) + dot_nt(along(cot_columns[:, SIDE:]), jnp.concatenate([rest, rest, right], axis=0))
    grads[0:CH, 0 : 3 * CH] = grads[0:CH, 0 : 3 * CH] + dot_nt(
        cc[CH : 2 * CH, 2 * SIDE : 3 * SIDE], hh[:, 0:SIDE]
    )
    grads[2 * CH :, 0 : 3 * CH] = grads[2 * CH :, 0 : 3 * CH] + dot_nt(
        cc[CH : 2 * CH, (SIDE + 1) * SIDE : (SIDE + 2) * SIDE], hh[:, (SIDE + 1) * SIDE :]
    )

    share = red_src.shape[1]
    pieces = 3 * CH // share
    for half in range(2):
        for k in range(pieces):
            red_src[half * pieces + k] = grads[
                k * share : (k + 1) * share, half * SIDE : (half + 1) * SIDE
            ]
    for k in range(2 * pieces, group):
        red_src[k] = jnp.zeros((share, SIDE), F32)

    def part_copy(peer, place):
        return pltpu.make_async_remote_copy(
            src_ref=red_src.at[peer],
            dst_ref=red_in.at[place],
            send_sem=part_send.at[peer],
            recv_sem=part_recv.at[place],
            device_id=member(peer),
            device_id_type=MESH,
        )

    def sum_copy(peer, place):
        return pltpu.make_async_remote_copy(
            src_ref=red_out.at[place],
            dst_ref=red_out.at[place],
            send_sem=sum_send.at[peer],
            recv_sem=sum_recv.at[place],
            device_id=member(peer),
            device_id_type=MESH,
        )

    def each_member(act):
        def go(k, carry):
            act((flat + k) % group)
            return carry

        lax.fori_loop(1, group, go, 0)

    red_in[flat] = red_src[flat]
    each_member(lambda peer: part_copy(peer, flat).start())

    def hidden_halo(step, carry):
        at = cells(step, 1)
        hh[0:CH, at] = (hh[0:CH, at].astype(F32) + dot(left, west(step))).astype(BF16)
        hh[2 * CH :, at] = (hh[2 * CH :, at].astype(F32) + dot(right, east(step))).astype(BF16)
        return carry

    lax.fori_loop(0, STEPS, hidden_halo, 0)

    def forward_second(step, carry):
        term = dot(w_fwd_ref[...], hh[:, cells(step, 0, ROWS + 2)])
        out_vmem[:, cells(step)] = (
            term[0:CH, 0:STEP]
            + term[CH : 2 * CH, SIDE : SIDE + STEP]
            + term[2 * CH :, 2 * SIDE :]
        ).astype(BF16)
        out_copy(step).start()
        return carry

    lax.fori_loop(0, STEPS // 2, forward_second, 0)
    each_member(lambda peer: part_copy(peer, peer).wait_recv())
    total = lax.fori_loop(
        0, group, lambda k, acc: acc + red_in[k], jnp.zeros((share, SIDE), F32)
    )
    red_out[flat] = total * scale
    each_member(lambda peer: sum_copy(peer, flat).start())
    lax.fori_loop(STEPS // 2, STEPS, forward_second, 0)
    each_member(lambda peer: sum_copy(peer, peer).wait_recv())

    halves = [
        jnp.concatenate([red_out[half * pieces + k] for k in range(pieces)], axis=0)
        for half in range(2)
    ]
    turned = halves[1][0:SIDE].T
    for a in range(3):
        rows = slice(a * CH, (a + 1) * CH)
        gsecond_ref[3 * a] = halves[0][rows, 0:CH]
        gsecond_ref[3 * a + 1] = halves[0][rows, CH : 2 * CH]
        gsecond_ref[3 * a + 2] = halves[1][rows, 0:CH]
        for b in range(3):
            lane = 64 + a * 16 + b * 4
            gfirst_ref[3 * a + b] = turned[lane : lane + CIN, 0:CH]

    for part in (px, rim, inp, hid):
        finish(*part)
    each_member(lambda peer: part_copy(peer, flat).wait_send())
    each_member(lambda peer: sum_copy(peer, flat).wait_send())

    def written(step, carry):
        ghid_copy(step).wait()
        out_copy(step).wait()
        return carry

    lax.fori_loop(0, STEPS, written, 0)


def deliver(*refs):
    half = (len(refs) - 1) // 2
    sem = refs[-1]
    copies = []
    for src, dst in zip(refs[:half], refs[half : 2 * half]):
        if src.shape[-1] == PIX:
            for k in range(8):
                at = (0, pl.ds(k // 2 * 16, 16), pl.ds(k % 2 * (PIX // 2), PIX // 2))
                copies.append((src.at[at], dst.at[at]))
        else:
            copies.append((src, dst))
    started = [pltpu.make_async_copy(a, b, sem.at[n]) for n, (a, b) in enumerate(copies)]
    for copy in started:
        copy.start()
    for copy in started:
        copy.wait()


def body(cycle_maps, send_pick, recv_pick, neighbour, facing, conv_first, conv_second, cotangent):
    tile_count = lax.axis_size("tile")
    chan_count = lax.axis_size("chan")
    sub_count = lax.axis_size("sub")
    group = tile_count * chan_count * sub_count
    cap = send_pick.shape[0] // tile_count
    scale = 1.0 / math.sqrt(group * PIX)
    per_block = cap // SLOT_DEPTH
    block_rows = -(-CIN * per_block // 16) * 16
    share = 8 * -(-2 * 3 * CH // (8 * group))
    vmem = pl.BlockSpec(memory_space=pltpu.VMEM)
    smem = pl.BlockSpec(memory_space=pltpu.SMEM)
    dma = pltpu.SemaphoreType.DMA
    hbm = pl.BlockSpec(memory_space=pl.ANY)
    shapes = (
        jax.ShapeDtypeStruct((1, CH, PIX), BF16),
        jax.ShapeDtypeStruct((1, CH, PIX), BF16),
        jax.ShapeDtypeStruct((9, CIN, CH), F32),
        jax.ShapeDtypeStruct((9, CH, CH), F32),
    )
    results = pl.pallas_call(
        functools.partial(kernel, tile_count, chan_count, sub_count, cap, scale),
        out_shape=shapes,
        in_specs=[vmem, vmem, vmem, smem, smem, vmem, vmem, hbm],
        out_specs=(hbm, hbm, vmem, vmem),
        scratch_shapes=[
            pltpu.VMEM((CH, 48), BF16),
            pltpu.VMEM((3 * CH, 3 * CH), BF16),
            pltpu.VMEM((3 * CH, 3 * CH), BF16),
            pltpu.VMEM((2 * SIDE, 2 * SIDE), F32),
            pltpu.VMEM((CIN * PIX // SEND_DEPTH, SEND_DEPTH), F32),
            pltpu.VMEM((CIN * PIX // SEND_DEPTH, SEND_DEPTH), BF16),
            pltpu.VMEM((CH, PIX), BF16),
            pltpu.VMEM((CH, PIX), BF16),
            pltpu.VMEM((CH, PIX), BF16),
            pltpu.VMEM((4 * SIDE, STEP), BF16),
            pltpu.VMEM((3 * CH, (SIDE + 4) * SIDE), BF16),
            pltpu.VMEM((3 * CH, (SIDE + 2) * SIDE), BF16),
            pltpu.VMEM((16, (SIDE + 2) * SIDE), BF16),
            pltpu.VMEM((8, PIX), F32),
            pltpu.VMEM((CH, PIX), F32),
            pltpu.VMEM((CH, PIX), F32),
            pltpu.VMEM((3 * CH, 2 * SIDE), F32),
            pltpu.VMEM((tile_count, block_rows, SLOT_DEPTH), F32),
            pltpu.VMEM((tile_count, block_rows, SLOT_DEPTH), BF16),
            pltpu.VMEM((tile_count, block_rows, SLOT_DEPTH), BF16),
            pltpu.VMEM((tile_count, 4, 16, SIDE), BF16),
            pltpu.VMEM((tile_count, 4, CH, SIDE), BF16),
            pltpu.VMEM((tile_count, 4, CH, SIDE), BF16),
            pltpu.VMEM((group, share, SIDE), F32),
            pltpu.VMEM((group, share, SIDE), F32),
            pltpu.VMEM((group, share, SIDE), F32),
        ]
        + [dma((tile_count,))] * 8
        + [dma((group,))] * 4
        + [dma(()), dma((STEPS,)), dma((STEPS,))],
        compiler_params=pltpu.CompilerParams(
            collective_id=0, has_side_effects=True, vmem_limit_bytes=56 * 1024 * 1024
        ),
        cost_estimate=pl.CostEstimate(
            flops=6_000_000_000, bytes_accessed=8_000_000, transcendentals=1_000_000
        ),
    )(
        cycle_maps,
        send_pick.reshape(1, -1),
        recv_pick.reshape(1, -1),
        neighbour,
        facing,
        conv_first.transpose(0, 2, 1),
        conv_second,
        cotangent,
    )
    out, ghid, gfirst, gsecond = pl.pallas_call(
        deliver,
        out_shape=shapes,
        in_specs=[hbm] * 4,
        out_specs=(hbm,) * 4,
        scratch_shapes=[dma((18,))],
        compiler_params=pltpu.CompilerParams(vmem_limit_bytes=56 * 1024 * 1024),
    )(*results)
    return out, ghid, gfirst.transpose(0, 2, 1), gsecond


def solution(mesh):
    in_specs = (
        P(("groups", "chan", "sub"), None, "tile"),
        P("tile"),
        P("tile"),
        P(),
        P(),
        P(),
        P(),
        P(("groups", "chan", "sub"), None, "tile"),
    )
    out_specs = (
        P(("groups", "chan", "sub"), None, "tile"),
        P(("groups", "chan", "sub"), None, "tile"),
        P("groups", None, None),
        P("groups", None, None),
    )
    return jax.shard_map(body, mesh=mesh, in_specs=in_specs, out_specs=out_specs, check_vma=False)
```

```python
import functools
import math

import jax
import jax.numpy as jnp
from jax import lax
from jax.experimental import pallas as pl
from jax.experimental.pallas import tpu as pltpu
from jax.sharding import PartitionSpec as P

SIDE = 128
CH = 64
CIN = 3
PIX = SIDE * SIDE
ROWS = 16
STEP = ROWS * SIDE
STEPS = SIDE // ROWS
SEND_DEPTH = 256
SLOT_DEPTH = 384
MESH = pl.DeviceIdType.MESH
F32 = jnp.float32
BF16 = jnp.bfloat16
NT = (((1,), (1,)), ((), ()))
TN = (((0,), (0,)), ((), ()))


def dot(a, b):
    return jnp.dot(a, b, preferred_element_type=F32)


def dot_nt(a, b):
    return lax.dot_general(a, b, NT, preferred_element_type=F32)


def dot_tn(a, b):
    return lax.dot_general(a, b, TN, preferred_element_type=F32)


def lane_is(x, lane):
    kind = jnp.int16 if x.dtype == BF16 else jnp.int32
    return lax.broadcasted_iota(kind, (x.shape[0], SIDE), 1) == lane


def tile_rows(x):
    return [x[:, r * SIDE : (r + 1) * SIDE] for r in range(x.shape[1] // SIDE)]


def turn(x, amount):
    return x if isinstance(amount, int) and amount % SIDE == 0 else pltpu.roll(x, amount, 1)


def west_edge(rows, fill):
    return [
        jnp.where(lane_is(row, 0), jnp.zeros_like(row) if fill is None else turn(fill, (SIDE - r) % SIDE), row)
        for r, row in enumerate(rows)
    ]


def east_edge(rows, fill):
    return [
        jnp.where(lane_is(row, SIDE - 1), jnp.zeros_like(row) if fill is None else turn(fill, SIDE - 1 - r), row)
        for r, row in enumerate(rows)
    ]


def from_left(x, fill=None):
    rows = [pltpu.roll(row, 1, 1) for row in tile_rows(x)]
    return jnp.concatenate(west_edge(rows, fill), axis=1).astype(x.dtype)


def from_right(x, fill=None):
    rows = [pltpu.roll(row, SIDE - 1, 1) for row in tile_rows(x)]
    return jnp.concatenate(east_edge(rows, fill), axis=1).astype(x.dtype)


def unwind(strip, step):
    return pltpu.roll(strip, (SIDE - ROWS * step) % SIDE, 1)


def pick_edges(x, step):
    first = jnp.zeros((x.shape[0], SIDE), x.dtype)
    last = first
    for r, row in enumerate(tile_rows(x)):
        here = lane_is(row, r)
        first = jnp.where(here, turn(row, r), first)
        last = jnp.where(here, turn(row, r + 1), last)
    return pltpu.roll(first, ROWS * step, 1), pltpu.roll(last, ROWS * step, 1)


def add_edges(total, x, step):
    first, last = pick_edges(x, step)
    return total[0] + first, total[1] + last


def loop(low, high, act, carry=0, unroll=2):
    def several(k, carry):
        for u in range(unroll):
            carry = act(low + k * unroll + u, carry)
        return carry

    return lax.fori_loop(0, (high - low) // unroll, several, carry)


def one_hot(depth, index):
    shape = (depth, index.shape[1])
    position = lax.broadcasted_iota(jnp.int16, shape, 0)
    hit = position == index.astype(jnp.int16)
    return jnp.where(hit, jnp.ones(shape, BF16), jnp.zeros(shape, BF16))


def kernel(
    tile_count,
    chan_count,
    sub_count,
    cap,
    scale,
    cycle_ref,
    send_ref,
    recv_ref,
    nbr_ref,
    face_ref,
    first_ref,
    second_ref,
    cot_hbm,
    out_ref,
    ghid_ref,
    gfirst_ref,
    gsecond_ref,
    w_first_ref,
    w_fwd_ref,
    w_bwd_ref,
    weights,
    table_wide,
    table_ref,
    cot_ref,
    out_vmem,
    ghid_vmem,
    cc,
    hh,
    xx,
    tiles,
    slope,
    hgrad,
    grads,
    slots,
    block_out,
    block_in,
    strip_in,
    strip_hid,
    strip_rim,
    red_src,
    red_in,
    red_out,
    px_send,
    px_recv,
    in_send,
    in_recv,
    hid_send,
    hid_recv,
    rim_send,
    rim_recv,
    part_send,
    part_recv,
    sum_send,
    sum_recv,
    cot_sem,
    out_sem,
    ghid_sem,
):
    me = lax.axis_index("tile")
    group = tile_count * chan_count * sub_count
    flat = (me * chan_count + lax.axis_index("chan")) * sub_count + lax.axis_index("sub")
    groups_per_block = cap // SLOT_DEPTH
    block_rows = block_out.shape[1]

    def member(index):
        return {
            "tile": index // (chan_count * sub_count),
            "chan": (index // sub_count) % chan_count,
            "sub": index % sub_count,
        }

    barrier = pltpu.get_barrier_semaphore()

    def greet(k, carry):
        pl.semaphore_signal(
            barrier, inc=1, device_id=member((flat + k) % group), device_id_type=MESH
        )
        return carry

    lax.fori_loop(1, group, greet, 0)
    cot_copy = pltpu.make_async_copy(cot_hbm.at[0], cot_ref, cot_sem)
    cot_copy.start()

    for a in range(3):
        for b in range(3):
            weights[a * CH : (a + 1) * CH, b * CH : (b + 1) * CH] = second_ref[
                3 * a + b
            ].astype(F32)
    w_fwd_ref[...] = weights[0 : 3 * CH, 0 : 3 * CH].astype(BF16)
    weights[...] = jnp.zeros_like(weights)
    for a in range(3):
        for b in range(3):
            weights[b * CH : (b + 1) * CH, a * CH : (a + 1) * CH] = second_ref[
                3 * a + b
            ].astype(F32)
    w_bwd_ref[...] = weights[...].T[0 : 3 * CH, 0 : 3 * CH].astype(BF16)
    weights[0:SIDE, 0:SIDE] = jnp.zeros((SIDE, SIDE), F32)
    for a in range(3):
        for b in range(3):
            at = a * 16 + b * 4
            weights[at : at + CIN, 0:CH] = first_ref[3 * a + b].astype(F32)
    w_first_ref[...] = weights[0:SIDE, 0:SIDE].T[0:CH, 0:48].astype(BF16)
    for g in range(PIX // SEND_DEPTH):
        piece = cycle_ref[0, :, g * SEND_DEPTH : (g + 1) * SEND_DEPTH].astype(F32)
        for c in range(CIN):
            row = c * (PIX // SEND_DEPTH) + g
            table_wide[row : row + 1, :] = piece[c : c + 1]
    table_ref[...] = table_wide[...].astype(BF16)

    def tile_copy(src, dst, send_sem, recv_sem, peer, place):
        return pltpu.make_async_remote_copy(
            src_ref=src,
            dst_ref=dst.at[place],
            send_sem=send_sem.at[peer],
            recv_sem=recv_sem.at[place],
            device_id={"tile": peer},
            device_id_type=MESH,
        )

    def post(source, dst, send_sem, recv_sem):
        def go(k, carry):
            peer = (me + k) % tile_count
            tile_copy(source(peer), dst, send_sem, recv_sem, peer, me).start()
            return carry

        lax.fori_loop(1, tile_count, go, 0)

    def collect(source, dst, send_sem, recv_sem):
        def go(k, carry):
            peer = (me + k) % tile_count
            tile_copy(source(peer), dst, send_sem, recv_sem, peer, peer).wait_recv()
            return carry

        lax.fori_loop(1, tile_count, go, 0)

    def finish(source, dst, send_sem, recv_sem):
        def go(k, carry):
            peer = (me + k) % tile_count
            tile_copy(source(peer), dst, send_sem, recv_sem, peer, me).wait_send()
            return carry

        lax.fori_loop(1, tile_count, go, 0)

    px = (lambda peer: block_out.at[peer], block_in, px_send, px_recv)
    inp = (lambda peer: strip_in.at[me], strip_in, in_send, in_recv)
    hid = (lambda peer: strip_hid.at[me], strip_hid, hid_send, hid_recv)
    rim = (lambda peer: strip_rim.at[me], strip_rim, rim_send, rim_recv)

    flip = jnp.where(
        lax.broadcasted_iota(jnp.int32, (SIDE, SIDE), 0)
        + lax.broadcasted_iota(jnp.int32, (SIDE, SIDE), 1)
        == SIDE - 1,
        1.0,
        0.0,
    ).astype(BF16)

    def reverse(strip):
        return dot(strip.astype(BF16), flip)

    def cells(step, extra=0, rows=ROWS):
        return pl.ds(pl.multiple_of(step * STEP + extra * SIDE, SIDE), rows * SIDE)

    if block_rows != CIN * groups_per_block:
        slots[...] = jnp.zeros_like(slots)
    quads = groups_per_block // 4
    width = 4 * SLOT_DEPTH
    table_groups = PIX // SEND_DEPTH

    def fill(it, carry):
        pick = send_ref[0:1, pl.ds(pl.multiple_of(it * width, SIDE), width)]
        hot = one_hot(SEND_DEPTH, pick & (SEND_DEPTH - 1))
        found = dot(table_ref[...], hot)
        mask = lax.broadcasted_iota(jnp.int32, (table_groups, width), 0) == pick // SEND_DEPTH
        dest = it // quads
        first = (it % quads) * 4
        for c in range(CIN):
            part = found[c * table_groups : (c + 1) * table_groups]
            value = jnp.sum(jnp.where(mask, part, 0.0), axis=0, keepdims=True)
            for q in range(4):
                slots[dest, pl.ds(c * groups_per_block + first + q, 1), :] = value[
                    :, q * SLOT_DEPTH : (q + 1) * SLOT_DEPTH
                ]
        return carry

    loop(0, tile_count * quads, fill)
    block_out[...] = slots[...].astype(BF16)
    block_in[me] = block_out[me]
    pl.semaphore_wait(barrier, group - 1)
    post(*px)

    cc[:, 0 : 2 * SIDE] = jnp.zeros((3 * CH, 2 * SIDE), BF16)
    cc[:, (SIDE + 2) * SIDE : (SIDE + 4) * SIDE] = jnp.zeros((3 * CH, 2 * SIDE), BF16)

    cot_copy.wait()

    def shift_cotangent(step, columns):
        narrow = cot_ref[:, cells(step)]
        at = cells(step, 2)
        cc[0:CH, at] = from_right(narrow)
        cc[CH : 2 * CH, at] = narrow
        cc[2 * CH : 3 * CH, at] = from_left(narrow)
        return add_edges(columns, narrow, step)

    none = jnp.zeros((CH, SIDE), BF16)
    cot_columns = loop(0, STEPS, shift_cotangent, (none, none))

    def interior(step, carry):
        term = dot(w_bwd_ref[...], cc[:, cells(step, 1, ROWS + 2)])
        hgrad[:, cells(step)] = (
            term[0:CH, 2 * SIDE :]
            + term[CH : 2 * CH, SIDE : SIDE + STEP]
            + term[2 * CH :, 0:STEP]
        )
        return carry

    loop(0, STEPS // 2, interior)

    collect(*px)
    chunk = 1024

    def place(it, carry):
        at = pl.ds(pl.multiple_of(it * chunk, chunk), chunk)
        pick = recv_ref[0:1, at]
        key = ((pick // SIDE) * 171) // 512
        hot = one_hot(SLOT_DEPTH, pick - key * SLOT_DEPTH)
        table = block_in[...].reshape(tile_count * block_rows, SLOT_DEPTH)
        found = dot(table, hot)
        total = [jnp.zeros((groups_per_block, chunk), F32)] * CIN
        local = lax.broadcasted_iota(jnp.int32, (groups_per_block, chunk), 0)
        for owner in range(tile_count):
            mask = local + owner * groups_per_block == key
            for c in range(CIN):
                start = owner * block_rows + c * groups_per_block
                part = found[start : start + groups_per_block]
                total[c] = total[c] + jnp.where(mask, part, 0.0)
        row = lax.broadcasted_iota(jnp.int32, (8, chunk), 0)
        value = jnp.zeros((8, chunk), F32)
        for c in range(CIN):
            value = jnp.where(row == c, jnp.sum(total[c], axis=0, keepdims=True), value)
        tiles[:, at] = value
        return carry

    loop(0, PIX // chunk, place)

    def tall(x):
        return jnp.concatenate([x, jnp.zeros_like(x)], axis=0)

    def tile_columns(step, total):
        return add_edges(total, tiles[:, cells(step)], step)

    blank = jnp.zeros((8, SIDE), F32)
    columns = loop(0, STEPS, tile_columns, (blank, blank))
    strip_in[me, 0] = tall(tiles[:, 0:SIDE]).astype(BF16)
    strip_in[me, 1] = tall(columns[1]).astype(BF16)
    strip_in[me, 2] = reverse(tall(tiles[:, PIX - SIDE : PIX])).astype(BF16)
    strip_in[me, 3] = reverse(tall(columns[0])).astype(BF16)
    post(*inp)

    def along(column):
        return jnp.concatenate([from_right(column), column, from_left(column)], axis=0)

    def outer(b):
        return jnp.concatenate([second_ref[3 * a + b] for a in range(3)], axis=0)

    strip_rim[me, 0] = dot(w_bwd_ref[0:CH, :], cc[:, 2 * SIDE : 3 * SIDE]).astype(BF16)
    strip_rim[me, 1] = dot_tn(outer(2), along(cot_columns[1])).astype(BF16)
    south = dot(w_bwd_ref[2 * CH :, :], cc[:, (SIDE + 1) * SIDE : (SIDE + 2) * SIDE])
    strip_rim[me, 2] = reverse(south).astype(BF16)
    strip_rim[me, 3] = reverse(dot_tn(outer(0), along(cot_columns[0]))).astype(BF16)
    post(*rim)

    loop(STEPS // 2, STEPS, interior)

    def incoming(buffer):
        strips = []
        for k in range(4):
            near = nbr_ref[me, k]
            there = jnp.where(near >= 0, 1.0, 0.0)
            strip = buffer[jnp.maximum(near, 0), face_ref[me, k]].astype(F32) * there
            strips.append(reverse(strip) if k < 2 else strip)
        return strips

    collect(*inp)
    north, right, bottom, left = incoming(strip_in)

    def three(mid, first, last):
        a = from_left(mid, first)
        b = from_right(mid, last)
        return jnp.concatenate([a + pltpu.roll(mid, 4, 0), b], axis=0).astype(BF16)

    xx[:, 0:SIDE] = three(north[0:8], None, None)
    xx[:, (SIDE + 1) * SIDE :] = three(bottom[0:8], None, None)
    left, right = left[0:8], right[0:8]

    def input_copies(step, carry):
        xx[:, cells(step, 1)] = three(
            tiles[:, cells(step)], unwind(left, step), unwind(right, step)
        )
        return carry

    loop(0, STEPS, input_copies)

    def input_stack(step):
        part = xx[:, cells(step, 0, ROWS + 2)]
        return [part[:, a * SIDE : a * SIDE + STEP] for a in range(3)]

    def forward_first(step, columns):
        pre = dot(w_first_ref[...], jnp.concatenate(input_stack(step), axis=0))
        sigma = jax.nn.sigmoid(pre)
        value = pre * sigma
        slope[:, cells(step)] = sigma * (1.0 + pre * (1.0 - sigma))
        narrow = value.astype(BF16)
        at = cells(step, 1)
        hh[0:CH, at] = from_left(narrow)
        hh[CH : 2 * CH, at] = narrow
        hh[2 * CH : 3 * CH, at] = from_right(narrow)
        return add_edges(columns, narrow, step)

    columns = loop(0, STEPS, forward_first, (none, none))
    strip_hid[me, 0] = hh[CH : 2 * CH, SIDE : 2 * SIDE]
    strip_hid[me, 1] = columns[1]
    strip_hid[me, 2] = reverse(hh[CH : 2 * CH, PIX : PIX + SIDE]).astype(BF16)
    strip_hid[me, 3] = reverse(columns[0]).astype(BF16)
    post(*hid)

    collect(*rim)
    north, right, bottom, left = incoming(strip_rim)
    hgrad[:, 0:SIDE] = hgrad[:, 0:SIDE] + north
    hgrad[:, PIX - SIDE : PIX] = hgrad[:, PIX - SIDE : PIX] + bottom
    rim_west, rim_east = left, right
    grads[...] = jnp.zeros_like(grads)

    def ghid_copy(step):
        at = cells(step)
        return pltpu.make_async_copy(ghid_vmem.at[:, at], ghid_ref.at[0, :, at], ghid_sem.at[step])

    def out_copy(step):
        at = cells(step)
        return pltpu.make_async_copy(out_vmem.at[:, at], out_ref.at[0, :, at], out_sem.at[step])

    def backward_first(step, carry):
        rows = tile_rows(hgrad[:, cells(step)])
        first, last = unwind(rim_west, step), unwind(rim_east, step)
        empty = [jnp.zeros((CH, SIDE), F32)] * ROWS
        edges = east_edge(west_edge(empty, first), last)
        total = jnp.concatenate([row + edge for row, edge in zip(rows, edges)], axis=1)
        ghid_vmem[:, cells(step)] = total.astype(BF16)
        ghid_copy(step).start()
        pre_grad = (total * slope[:, cells(step)]).astype(BF16)
        stack = jnp.concatenate(
            [jnp.zeros((64, STEP), BF16)] + input_stack(step) + [jnp.zeros((16, STEP), BF16)],
            axis=0,
        )
        grads[0:CH, SIDE : 2 * SIDE] = grads[0:CH, SIDE : 2 * SIDE] + dot_nt(pre_grad, stack)
        return carry

    def backward_second(step, carry):
        part = cc[CH : 2 * CH, cells(step, 1, ROWS + 2)]
        rows = jnp.concatenate(
            [part[:, 2 * SIDE :], part[:, SIDE : SIDE + STEP], part[:, 0:STEP]], axis=0
        )
        grads[:, 0 : 3 * CH] = grads[:, 0 : 3 * CH] + dot_nt(rows, hh[:, cells(step, 1)])
        return carry

    loop(0, STEPS, lambda step, carry: backward_second(step, backward_first(step, carry)))
    collect(*hid)
    north, right, bottom, left = incoming(strip_hid)

    def halo_row(strip):
        return jnp.concatenate([from_left(strip), strip, from_right(strip)], axis=0).astype(BF16)

    hh[:, 0:SIDE] = halo_row(north)
    hh[:, (SIDE + 1) * SIDE :] = halo_row(bottom)
    left = left.astype(BF16)
    right = right.astype(BF16)
    rest = jnp.zeros((CH, SIDE), BF16)
    grads[:, 0 : 3 * CH] = grads[:, 0 : 3 * CH] + dot_nt(
        along(cot_columns[0]), jnp.concatenate([left, rest, rest], axis=0)
    ) + dot_nt(along(cot_columns[1]), jnp.concatenate([rest, rest, right], axis=0))
    grads[0:CH, 0 : 3 * CH] = grads[0:CH, 0 : 3 * CH] + dot_nt(
        cc[CH : 2 * CH, 2 * SIDE : 3 * SIDE], hh[:, 0:SIDE]
    )
    grads[2 * CH :, 0 : 3 * CH] = grads[2 * CH :, 0 : 3 * CH] + dot_nt(
        cc[CH : 2 * CH, (SIDE + 1) * SIDE : (SIDE + 2) * SIDE], hh[:, (SIDE + 1) * SIDE :]
    )

    share = red_src.shape[1]
    pieces = 3 * CH // share
    for half in range(2):
        for k in range(pieces):
            red_src[half * pieces + k] = grads[
                k * share : (k + 1) * share, half * SIDE : (half + 1) * SIDE
            ]
    for k in range(2 * pieces, group):
        red_src[k] = jnp.zeros((share, SIDE), F32)

    def part_copy(peer, place):
        return pltpu.make_async_remote_copy(
            src_ref=red_src.at[peer],
            dst_ref=red_in.at[place],
            send_sem=part_send.at[peer],
            recv_sem=part_recv.at[place],
            device_id=member(peer),
            device_id_type=MESH,
        )

    def sum_copy(peer, place):
        return pltpu.make_async_remote_copy(
            src_ref=red_out.at[place],
            dst_ref=red_out.at[place],
            send_sem=sum_send.at[peer],
            recv_sem=sum_recv.at[place],
            device_id=member(peer),
            device_id_type=MESH,
        )

    def each_member(act):
        def go(k, carry):
            act((flat + k) % group)
            return carry

        lax.fori_loop(1, group, go, 0)

    red_in[flat] = red_src[flat]
    each_member(lambda peer: part_copy(peer, flat).start())

    def hidden_halo(step, carry):
        at = cells(step, 1)
        first = west_edge(tile_rows(hh[0:CH, at]), unwind(left, step))
        last = east_edge(tile_rows(hh[2 * CH :, at]), unwind(right, step))
        hh[0:CH, at] = jnp.concatenate(first, axis=1)
        hh[2 * CH :, at] = jnp.concatenate(last, axis=1)
        return carry

    loop(0, STEPS, hidden_halo)

    def forward_second(step, carry):
        term = dot(w_fwd_ref[...], hh[:, cells(step, 0, ROWS + 2)])
        out_vmem[:, cells(step)] = (
            term[0:CH, 0:STEP]
            + term[CH : 2 * CH, SIDE : SIDE + STEP]
            + term[2 * CH :, 2 * SIDE :]
        ).astype(BF16)
        out_copy(step).start()
        return carry

    loop(0, STEPS // 2, forward_second)
    each_member(lambda peer: part_copy(peer, peer).wait_recv())
    total = lax.fori_loop(
        0, group, lambda k, acc: acc + red_in[k], jnp.zeros((share, SIDE), F32)
    )
    red_out[flat] = total * scale
    each_member(lambda peer: sum_copy(peer, flat).start())
    loop(STEPS // 2, STEPS, forward_second)
    each_member(lambda peer: sum_copy(peer, peer).wait_recv())

    halves = [
        jnp.concatenate([red_out[half * pieces + k] for k in range(pieces)], axis=0)
        for half in range(2)
    ]
    turned = halves[1][0:SIDE].T
    for a in range(3):
        rows = slice(a * CH, (a + 1) * CH)
        gsecond_ref[3 * a] = halves[0][rows, 0:CH]
        gsecond_ref[3 * a + 1] = halves[0][rows, CH : 2 * CH]
        gsecond_ref[3 * a + 2] = halves[1][rows, 0:CH]
        for b in range(3):
            lane = 64 + a * 16 + b * 4
            gfirst_ref[3 * a + b] = turned[lane : lane + CIN, 0:CH]

    for part in (px, rim, inp, hid):
        finish(*part)
    each_member(lambda peer: part_copy(peer, flat).wait_send())
    each_member(lambda peer: sum_copy(peer, flat).wait_send())

    def written(step, carry):
        ghid_copy(step).wait()
        out_copy(step).wait()
        return carry

    lax.fori_loop(0, STEPS, written, 0)


def deliver(*refs):
    count = (len(refs) - 2) // 3
    read_sem, write_sem = refs[3 * count :]
    reads, writes = [], []
    for src, dst, hold in zip(refs[:count], refs[count : 2 * count], refs[2 * count : 3 * count]):
        parts = [()]
        if src.shape[-1] == PIX:
            parts = [(0, slice(None), pl.ds(k * STEP, STEP)) for k in range(STEPS)]
        for at in parts:
            a, b, c = (src.at[at], hold.at[at], dst.at[at]) if at else (src, hold, dst)
            reads.append(pltpu.make_async_copy(a, b, read_sem.at[len(reads)]))
            writes.append(pltpu.make_async_copy(b, c, write_sem.at[len(writes)]))
    for copy in reads:
        copy.start()
    for read, write in zip(reads, writes):
        read.wait()
        write.start()
    for copy in writes:
        copy.wait()


def body(cycle_maps, send_pick, recv_pick, neighbour, facing, conv_first, conv_second, cotangent):
    tile_count = lax.axis_size("tile")
    chan_count = lax.axis_size("chan")
    sub_count = lax.axis_size("sub")
    group = tile_count * chan_count * sub_count
    cap = send_pick.shape[0] // tile_count
    scale = 1.0 / math.sqrt(group * PIX)
    per_block = cap // SLOT_DEPTH
    block_rows = -(-CIN * per_block // 16) * 16
    share = 8 * -(-2 * 3 * CH // (8 * group))
    vmem = pl.BlockSpec(memory_space=pltpu.VMEM)
    smem = pl.BlockSpec(memory_space=pltpu.SMEM)
    dma = pltpu.SemaphoreType.DMA
    hbm = pl.BlockSpec(memory_space=pl.ANY)
    shapes = (
        jax.ShapeDtypeStruct((1, CH, PIX), BF16),
        jax.ShapeDtypeStruct((1, CH, PIX), BF16),
        jax.ShapeDtypeStruct((9, CIN, CH), F32),
        jax.ShapeDtypeStruct((9, CH, CH), F32),
    )
    results = pl.pallas_call(
        functools.partial(kernel, tile_count, chan_count, sub_count, cap, scale),
        out_shape=shapes,
        in_specs=[vmem, vmem, vmem, smem, smem, vmem, vmem, hbm],
        out_specs=(hbm, hbm, vmem, vmem),
        scratch_shapes=[
            pltpu.VMEM((CH, 48), BF16),
            pltpu.VMEM((3 * CH, 3 * CH), BF16),
            pltpu.VMEM((3 * CH, 3 * CH), BF16),
            pltpu.VMEM((2 * SIDE, 2 * SIDE), F32),
            pltpu.VMEM((CIN * PIX // SEND_DEPTH, SEND_DEPTH), F32),
            pltpu.VMEM((CIN * PIX // SEND_DEPTH, SEND_DEPTH), BF16),
            pltpu.VMEM((CH, PIX), BF16),
            pltpu.VMEM((CH, PIX), BF16),
            pltpu.VMEM((CH, PIX), BF16),
            pltpu.VMEM((3 * CH, (SIDE + 4) * SIDE), BF16),
            pltpu.VMEM((3 * CH, (SIDE + 2) * SIDE), BF16),
            pltpu.VMEM((16, (SIDE + 2) * SIDE), BF16),
            pltpu.VMEM((8, PIX), F32),
            pltpu.VMEM((CH, PIX), F32),
            pltpu.VMEM((CH, PIX), F32),
            pltpu.VMEM((3 * CH, 2 * SIDE), F32),
            pltpu.VMEM((tile_count, block_rows, SLOT_DEPTH), F32),
            pltpu.VMEM((tile_count, block_rows, SLOT_DEPTH), BF16),
            pltpu.VMEM((tile_count, block_rows, SLOT_DEPTH), BF16),
            pltpu.VMEM((tile_count, 4, 16, SIDE), BF16),
            pltpu.VMEM((tile_count, 4, CH, SIDE), BF16),
            pltpu.VMEM((tile_count, 4, CH, SIDE), BF16),
            pltpu.VMEM((group, share, SIDE), F32),
            pltpu.VMEM((group, share, SIDE), F32),
            pltpu.VMEM((group, share, SIDE), F32),
        ]
        + [dma((tile_count,))] * 8
        + [dma((group,))] * 4
        + [dma(()), dma((STEPS,)), dma((STEPS,))],
        compiler_params=pltpu.CompilerParams(
            collective_id=0, has_side_effects=True, vmem_limit_bytes=56 * 1024 * 1024
        ),
        cost_estimate=pl.CostEstimate(
            flops=6_000_000_000, bytes_accessed=8_000_000, transcendentals=1_000_000
        ),
    )(
        cycle_maps,
        send_pick.reshape(1, -1),
        recv_pick.reshape(1, -1),
        neighbour,
        facing,
        conv_first.transpose(0, 2, 1),
        conv_second,
        cotangent,
    )
    out, ghid, gfirst, gsecond = pl.pallas_call(
        deliver,
        out_shape=shapes,
        in_specs=[hbm] * 4,
        out_specs=(hbm,) * 4,
        scratch_shapes=[pltpu.VMEM(shape.shape, shape.dtype) for shape in shapes]
        + [dma((2 * STEPS + 2,))] * 2,
        compiler_params=pltpu.CompilerParams(vmem_limit_bytes=56 * 1024 * 1024),
    )(*results)
    return out, ghid, gfirst.transpose(0, 2, 1), gsecond


def solution(mesh):
    in_specs = (
        P(("groups", "chan", "sub"), None, "tile"),
        P("tile"),
        P("tile"),
        P(),
        P(),
        P(),
        P(),
        P(("groups", "chan", "sub"), None, "tile"),
    )
    out_specs = (
        P(("groups", "chan", "sub"), None, "tile"),
        P(("groups", "chan", "sub"), None, "tile"),
        P("groups", None, None),
        P("groups", None, None),
    )
    return jax.shard_map(body, mesh=mesh, in_specs=in_specs, out_specs=out_specs, check_vma=False)
```

```python
import functools
import math

import jax
import jax.numpy as jnp
from jax import lax
from jax.experimental import pallas as pl
from jax.experimental.pallas import tpu as pltpu
from jax.sharding import PartitionSpec as P

SIDE = 128
CH = 64
CIN = 3
PIX = SIDE * SIDE
ROWS = 16
STEP = ROWS * SIDE
STEPS = SIDE // ROWS
SEND_DEPTH = 256
SLOT_DEPTH = 384
VMEM_BYTES = 40 * 1024 * 1024
MESH = pl.DeviceIdType.MESH
F32 = jnp.float32
BF16 = jnp.bfloat16
NT = (((1,), (1,)), ((), ()))
TN = (((0,), (0,)), ((), ()))


def dot(a, b):
    return jnp.dot(a, b, preferred_element_type=F32)


def dot_nt(a, b):
    return lax.dot_general(a, b, NT, preferred_element_type=F32)


def dot_tn(a, b):
    return lax.dot_general(a, b, TN, preferred_element_type=F32)


def lane_is(x, lane):
    kind = jnp.int16 if x.dtype == BF16 else jnp.int32
    return lax.broadcasted_iota(kind, (x.shape[0], SIDE), 1) == lane


def tile_rows(x):
    return [x[:, r * SIDE : (r + 1) * SIDE] for r in range(x.shape[1] // SIDE)]


def turn(x, amount):
    return x if isinstance(amount, int) and amount % SIDE == 0 else pltpu.roll(x, amount, 1)


def west_edge(rows, fill):
    return [
        jnp.where(lane_is(row, 0), jnp.zeros_like(row) if fill is None else turn(fill, (SIDE - r) % SIDE), row)
        for r, row in enumerate(rows)
    ]


def east_edge(rows, fill):
    return [
        jnp.where(lane_is(row, SIDE - 1), jnp.zeros_like(row) if fill is None else turn(fill, SIDE - 1 - r), row)
        for r, row in enumerate(rows)
    ]


def from_left(x, fill=None):
    rows = [pltpu.roll(row, 1, 1) for row in tile_rows(x)]
    return jnp.concatenate(west_edge(rows, fill), axis=1).astype(x.dtype)


def from_right(x, fill=None):
    rows = [pltpu.roll(row, SIDE - 1, 1) for row in tile_rows(x)]
    return jnp.concatenate(east_edge(rows, fill), axis=1).astype(x.dtype)


def unwind(strip, step):
    return pltpu.roll(strip, (SIDE - ROWS * step) % SIDE, 1)


def pick_edges(x, step):
    first = jnp.zeros((x.shape[0], SIDE), x.dtype)
    last = first
    for r, row in enumerate(tile_rows(x)):
        here = lane_is(row, r)
        first = jnp.where(here, turn(row, r), first)
        last = jnp.where(here, turn(row, r + 1), last)
    return pltpu.roll(first, ROWS * step, 1), pltpu.roll(last, ROWS * step, 1)


def add_edges(total, x, step):
    first, last = pick_edges(x, step)
    return total[0] + first, total[1] + last


def loop(low, high, act, carry=0, unroll=4):
    def several(k, carry):
        for u in range(unroll):
            carry = act(low + k * unroll + u, carry)
        return carry

    return lax.fori_loop(0, (high - low) // unroll, several, carry)


def one_hot(depth, index):
    shape = (depth, index.shape[1])
    position = lax.broadcasted_iota(jnp.int16, shape, 0)
    hit = position == index.astype(jnp.int16)
    return jnp.where(hit, jnp.ones(shape, BF16), jnp.zeros(shape, BF16))


def kernel(
    tile_count,
    chan_count,
    sub_count,
    cap,
    scale,
    cycle_ref,
    send_ref,
    recv_ref,
    nbr_ref,
    face_ref,
    first_ref,
    second_ref,
    cot_hbm,
    out_ref,
    ghid_ref,
    gfirst_ref,
    gsecond_ref,
    w_first_ref,
    w_fwd_ref,
    w_bwd_ref,
    weights,
    table_wide,
    table_ref,
    cot_ref,
    cc,
    hh,
    xx,
    tiles,
    slope,
    hgrad,
    grads,
    slots,
    block_out,
    block_in,
    strip_in,
    strip_hid,
    strip_rim,
    red_src,
    red_in,
    red_out,
    px_send,
    px_recv,
    in_send,
    in_recv,
    hid_send,
    hid_recv,
    rim_send,
    rim_recv,
    part_send,
    part_recv,
    sum_send,
    sum_recv,
    cot_sem,
):
    me = lax.axis_index("tile")
    group = tile_count * chan_count * sub_count
    flat = (me * chan_count + lax.axis_index("chan")) * sub_count + lax.axis_index("sub")
    groups_per_block = cap // SLOT_DEPTH
    block_rows = block_out.shape[1]

    def member(index):
        return {
            "tile": index // (chan_count * sub_count),
            "chan": (index // sub_count) % chan_count,
            "sub": index % sub_count,
        }

    barrier = pltpu.get_barrier_semaphore()

    def greet(k, carry):
        pl.semaphore_signal(
            barrier, inc=1, device_id=member((flat + k) % group), device_id_type=MESH
        )
        return carry

    lax.fori_loop(1, group, greet, 0)
    cot_copy = pltpu.make_async_copy(cot_hbm.at[0], cot_ref, cot_sem)
    cot_copy.start()

    for g in range(PIX // SEND_DEPTH):
        piece = cycle_ref[0, :, g * SEND_DEPTH : (g + 1) * SEND_DEPTH].astype(F32)
        for c in range(CIN):
            row = c * (PIX // SEND_DEPTH) + g
            table_wide[row : row + 1, :] = piece[c : c + 1]
    table_ref[...] = table_wide[...].astype(BF16)

    def tile_copy(src, dst, send_sem, recv_sem, peer, place):
        return pltpu.make_async_remote_copy(
            src_ref=src,
            dst_ref=dst.at[place],
            send_sem=send_sem.at[peer],
            recv_sem=recv_sem.at[place],
            device_id={"tile": peer},
            device_id_type=MESH,
        )

    def post(source, dst, send_sem, recv_sem):
        def go(k, carry):
            peer = (me + k) % tile_count
            tile_copy(source(peer), dst, send_sem, recv_sem, peer, me).start()
            return carry

        lax.fori_loop(1, tile_count, go, 0)

    def collect(source, dst, send_sem, recv_sem):
        def go(k, carry):
            peer = (me + k) % tile_count
            tile_copy(source(peer), dst, send_sem, recv_sem, peer, peer).wait_recv()
            return carry

        lax.fori_loop(1, tile_count, go, 0)

    def finish(source, dst, send_sem, recv_sem):
        def go(k, carry):
            peer = (me + k) % tile_count
            tile_copy(source(peer), dst, send_sem, recv_sem, peer, me).wait_send()
            return carry

        lax.fori_loop(1, tile_count, go, 0)

    px = (lambda peer: block_out.at[peer], block_in, px_send, px_recv)
    inp = (lambda peer: strip_in.at[me], strip_in, in_send, in_recv)
    hid = (lambda peer: strip_hid.at[me], strip_hid, hid_send, hid_recv)
    rim = (lambda peer: strip_rim.at[me], strip_rim, rim_send, rim_recv)

    flip = jnp.where(
        lax.broadcasted_iota(jnp.int32, (SIDE, SIDE), 0)
        + lax.broadcasted_iota(jnp.int32, (SIDE, SIDE), 1)
        == SIDE - 1,
        1.0,
        0.0,
    ).astype(BF16)

    def reverse(strip):
        return dot(strip.astype(BF16), flip)

    def cells(step, extra=0, rows=ROWS):
        return pl.ds(pl.multiple_of(step * STEP + extra * SIDE, SIDE), rows * SIDE)

    if block_rows != CIN * groups_per_block:
        slots[...] = jnp.zeros_like(slots)
    quads = groups_per_block // 4
    width = 4 * SLOT_DEPTH
    table_groups = PIX // SEND_DEPTH

    def fill(dest, quad):
        at = (dest * quads + quad) * width
        pick = send_ref[0:1, pl.ds(pl.multiple_of(at, SIDE), width)]
        hot = one_hot(SEND_DEPTH, pick & (SEND_DEPTH - 1))
        found = dot(table_ref[...], hot)
        mask = lax.broadcasted_iota(jnp.int32, (table_groups, width), 0) == pick // SEND_DEPTH
        for c in range(CIN):
            part = found[c * table_groups : (c + 1) * table_groups]
            value = jnp.sum(jnp.where(mask, part, 0.0), axis=0, keepdims=True)
            for q in range(4):
                row = c * groups_per_block + quad * 4 + q
                slots[dest, row : row + 1, :] = value[:, q * SLOT_DEPTH : (q + 1) * SLOT_DEPTH]

    def fill_block(dest):
        for quad in range(quads):
            fill(dest, quad)
        block_out[dest] = slots[dest].astype(BF16)

    def send_block(k, carry):
        dest = (me + k) % tile_count
        fill_block(dest)
        tile_copy(px[0](dest), *px[1:], dest, me).start()
        return carry

    pl.semaphore_wait(barrier, group - 1)
    lax.fori_loop(1, tile_count, send_block, 0)
    fill_block(me)
    block_in[me] = block_out[me]

    for a in range(3):
        for b in range(3):
            weights[a * CH : (a + 1) * CH, b * CH : (b + 1) * CH] = second_ref[
                3 * a + b
            ].astype(F32)
    w_fwd_ref[...] = weights[0 : 3 * CH, 0 : 3 * CH].astype(BF16)
    weights[...] = jnp.zeros_like(weights)
    for a in range(3):
        for b in range(3):
            weights[b * CH : (b + 1) * CH, a * CH : (a + 1) * CH] = second_ref[
                3 * a + b
            ].astype(F32)
    w_bwd_ref[...] = weights[...].T[0 : 3 * CH, 0 : 3 * CH].astype(BF16)
    weights[0:SIDE, 0:SIDE] = jnp.zeros((SIDE, SIDE), F32)
    for a in range(3):
        for b in range(3):
            at = a * 16 + b * 4
            weights[at : at + CIN, 0:CH] = first_ref[3 * a + b].astype(F32)
    w_first_ref[...] = weights[0:SIDE, 0:SIDE].T[0:CH, 0:48].astype(BF16)
    cc[:, 0 : 2 * SIDE] = jnp.zeros((3 * CH, 2 * SIDE), BF16)
    cc[:, (SIDE + 2) * SIDE : (SIDE + 4) * SIDE] = jnp.zeros((3 * CH, 2 * SIDE), BF16)

    cot_copy.wait()

    def shift_cotangent(step, columns):
        narrow = cot_ref[:, cells(step)]
        at = cells(step, 2)
        cc[0:CH, at] = from_right(narrow)
        cc[CH : 2 * CH, at] = narrow
        cc[2 * CH : 3 * CH, at] = from_left(narrow)
        return add_edges(columns, narrow, step)

    none = jnp.zeros((CH, SIDE), BF16)
    cot_columns = loop(0, STEPS, shift_cotangent, (none, none))

    def interior(step, carry):
        term = dot(w_bwd_ref[...], cc[:, cells(step, 1, ROWS + 2)])
        hgrad[:, cells(step)] = (
            term[0:CH, 2 * SIDE :]
            + term[CH : 2 * CH, SIDE : SIDE + STEP]
            + term[2 * CH :, 0:STEP]
        )
        return carry

    loop(0, STEPS // 2, interior)

    collect(*px)
    chunk = 1024

    def place(it, carry):
        at = pl.ds(pl.multiple_of(it * chunk, chunk), chunk)
        pick = recv_ref[0:1, at]
        key = ((pick // SIDE) * 171) // 512
        hot = one_hot(SLOT_DEPTH, pick - key * SLOT_DEPTH)
        table = block_in[...].reshape(tile_count * block_rows, SLOT_DEPTH)
        found = dot(table, hot)
        total = [jnp.zeros((groups_per_block, chunk), F32)] * CIN
        local = lax.broadcasted_iota(jnp.int32, (groups_per_block, chunk), 0)
        for owner in range(tile_count):
            mask = local + owner * groups_per_block == key
            for c in range(CIN):
                start = owner * block_rows + c * groups_per_block
                part = found[start : start + groups_per_block]
                total[c] = total[c] + jnp.where(mask, part, 0.0)
        row = lax.broadcasted_iota(jnp.int32, (8, chunk), 0)
        value = jnp.zeros((8, chunk), F32)
        for c in range(CIN):
            value = jnp.where(row == c, jnp.sum(total[c], axis=0, keepdims=True), value)
        tiles[:, at] = value
        return carry

    loop(0, PIX // chunk, place)

    def tall(x):
        return jnp.concatenate([x, jnp.zeros_like(x)], axis=0)

    def tile_columns(step, total):
        return add_edges(total, tiles[:, cells(step)], step)

    blank = jnp.zeros((8, SIDE), F32)
    columns = loop(0, STEPS, tile_columns, (blank, blank))
    strip_in[me, 0] = tall(tiles[:, 0:SIDE]).astype(BF16)
    strip_in[me, 1] = tall(columns[1]).astype(BF16)
    strip_in[me, 2] = reverse(tall(tiles[:, PIX - SIDE : PIX])).astype(BF16)
    strip_in[me, 3] = reverse(tall(columns[0])).astype(BF16)
    post(*inp)

    def along(column):
        return jnp.concatenate([from_right(column), column, from_left(column)], axis=0)

    def outer(b):
        return jnp.concatenate([second_ref[3 * a + b] for a in range(3)], axis=0)

    strip_rim[me, 0] = dot(w_bwd_ref[0:CH, :], cc[:, 2 * SIDE : 3 * SIDE]).astype(BF16)
    strip_rim[me, 1] = dot_tn(outer(2), along(cot_columns[1])).astype(BF16)
    south = dot(w_bwd_ref[2 * CH :, :], cc[:, (SIDE + 1) * SIDE : (SIDE + 2) * SIDE])
    strip_rim[me, 2] = reverse(south).astype(BF16)
    strip_rim[me, 3] = reverse(dot_tn(outer(0), along(cot_columns[0]))).astype(BF16)
    post(*rim)

    loop(STEPS // 2, STEPS, interior)

    def incoming(buffer):
        strips = []
        for k in range(4):
            near = nbr_ref[me, k]
            there = jnp.where(near >= 0, 1.0, 0.0)
            strip = buffer[jnp.maximum(near, 0), face_ref[me, k]].astype(F32) * there
            strips.append(reverse(strip) if k < 2 else strip)
        return strips

    collect(*inp)
    north, right, bottom, left = incoming(strip_in)

    def three(mid, first, last):
        a = from_left(mid, first)
        b = from_right(mid, last)
        return jnp.concatenate([a + pltpu.roll(mid, 4, 0), b], axis=0).astype(BF16)

    xx[:, 0:SIDE] = three(north[0:8], None, None)
    xx[:, (SIDE + 1) * SIDE :] = three(bottom[0:8], None, None)
    left, right = left[0:8], right[0:8]

    def input_copies(step, carry):
        xx[:, cells(step, 1)] = three(
            tiles[:, cells(step)], unwind(left, step), unwind(right, step)
        )
        return carry

    loop(0, STEPS, input_copies)

    def input_stack(step):
        part = xx[:, cells(step, 0, ROWS + 2)]
        return [part[:, a * SIDE : a * SIDE + STEP] for a in range(3)]

    def forward_first(step, columns):
        pre = dot(w_first_ref[...], jnp.concatenate(input_stack(step), axis=0))
        sigma = jax.nn.sigmoid(pre)
        value = pre * sigma
        slope[:, cells(step)] = sigma * (1.0 + pre * (1.0 - sigma))
        narrow = value.astype(BF16)
        at = cells(step, 1)
        hh[0:CH, at] = from_left(narrow)
        hh[CH : 2 * CH, at] = narrow
        hh[2 * CH : 3 * CH, at] = from_right(narrow)
        return add_edges(columns, narrow, step)

    columns = loop(0, STEPS, forward_first, (none, none))
    strip_hid[me, 0] = hh[CH : 2 * CH, SIDE : 2 * SIDE]
    strip_hid[me, 1] = columns[1]
    strip_hid[me, 2] = reverse(hh[CH : 2 * CH, PIX : PIX + SIDE]).astype(BF16)
    strip_hid[me, 3] = reverse(columns[0]).astype(BF16)
    post(*hid)

    collect(*rim)
    north, right, bottom, left = incoming(strip_rim)
    hgrad[:, 0:SIDE] = hgrad[:, 0:SIDE] + north
    hgrad[:, PIX - SIDE : PIX] = hgrad[:, PIX - SIDE : PIX] + bottom
    rim_west, rim_east = left, right
    grads[...] = jnp.zeros_like(grads)

    def backward_first(step, carry):
        rows = tile_rows(hgrad[:, cells(step)])
        first, last = unwind(rim_west, step), unwind(rim_east, step)
        empty = [jnp.zeros((CH, SIDE), F32)] * ROWS
        edges = east_edge(west_edge(empty, first), last)
        total = jnp.concatenate([row + edge for row, edge in zip(rows, edges)], axis=1)
        ghid_ref[0, :, cells(step)] = total.astype(BF16)
        pre_grad = (total * slope[:, cells(step)]).astype(BF16)
        stack = jnp.concatenate(
            [jnp.zeros((64, STEP), BF16)] + input_stack(step) + [jnp.zeros((16, STEP), BF16)],
            axis=0,
        )
        grads[0:CH, SIDE : 2 * SIDE] = grads[0:CH, SIDE : 2 * SIDE] + dot_nt(pre_grad, stack)
        return carry

    def backward_second(step, carry):
        part = cc[CH : 2 * CH, cells(step, 1, ROWS + 2)]
        rows = jnp.concatenate(
            [part[:, 2 * SIDE :], part[:, SIDE : SIDE + STEP], part[:, 0:STEP]], axis=0
        )
        grads[:, 0 : 3 * CH] = grads[:, 0 : 3 * CH] + dot_nt(rows, hh[:, cells(step, 1)])
        return carry

    loop(0, STEPS, lambda step, carry: backward_second(step, backward_first(step, carry)))
    collect(*hid)
    north, right, bottom, left = incoming(strip_hid)

    def halo_row(strip):
        return jnp.concatenate([from_left(strip), strip, from_right(strip)], axis=0).astype(BF16)

    hh[:, 0:SIDE] = halo_row(north)
    hh[:, (SIDE + 1) * SIDE :] = halo_row(bottom)
    left = left.astype(BF16)
    right = right.astype(BF16)
    rest = jnp.zeros((CH, SIDE), BF16)
    grads[:, 0 : 3 * CH] = grads[:, 0 : 3 * CH] + dot_nt(
        along(cot_columns[0]), jnp.concatenate([left, rest, rest], axis=0)
    ) + dot_nt(along(cot_columns[1]), jnp.concatenate([rest, rest, right], axis=0))
    grads[0:CH, 0 : 3 * CH] = grads[0:CH, 0 : 3 * CH] + dot_nt(
        cc[CH : 2 * CH, 2 * SIDE : 3 * SIDE], hh[:, 0:SIDE]
    )
    grads[2 * CH :, 0 : 3 * CH] = grads[2 * CH :, 0 : 3 * CH] + dot_nt(
        cc[CH : 2 * CH, (SIDE + 1) * SIDE : (SIDE + 2) * SIDE], hh[:, (SIDE + 1) * SIDE :]
    )

    share = red_src.shape[1]
    pieces = 3 * CH // share
    for half in range(2):
        for k in range(pieces):
            red_src[half * pieces + k] = grads[
                k * share : (k + 1) * share, half * SIDE : (half + 1) * SIDE
            ]
    for k in range(2 * pieces, group):
        red_src[k] = jnp.zeros((share, SIDE), F32)

    def part_copy(peer, place):
        return pltpu.make_async_remote_copy(
            src_ref=red_src.at[peer],
            dst_ref=red_in.at[place],
            send_sem=part_send.at[peer],
            recv_sem=part_recv.at[place],
            device_id=member(peer),
            device_id_type=MESH,
        )

    def sum_copy(peer, place):
        return pltpu.make_async_remote_copy(
            src_ref=red_out.at[place],
            dst_ref=red_out.at[place],
            send_sem=sum_send.at[peer],
            recv_sem=sum_recv.at[place],
            device_id=member(peer),
            device_id_type=MESH,
        )

    def each_member(act):
        def go(k, carry):
            act((flat + k) % group)
            return carry

        lax.fori_loop(1, group, go, 0)

    red_in[flat] = red_src[flat]
    each_member(lambda peer: part_copy(peer, flat).start())

    def hidden_halo(step, carry):
        at = cells(step, 1)
        first = west_edge(tile_rows(hh[0:CH, at]), unwind(left, step))
        last = east_edge(tile_rows(hh[2 * CH :, at]), unwind(right, step))
        hh[0:CH, at] = jnp.concatenate(first, axis=1)
        hh[2 * CH :, at] = jnp.concatenate(last, axis=1)
        return carry

    hidden_halo(0, 0)

    def forward_second(step, carry, ahead=True):
        if ahead:
            hidden_halo(step + 1, 0)
        term = dot(w_fwd_ref[...], hh[:, cells(step, 0, ROWS + 2)])
        out_ref[0, :, cells(step)] = (
            term[0:CH, 0:STEP]
            + term[CH : 2 * CH, SIDE : SIDE + STEP]
            + term[2 * CH :, 2 * SIDE :]
        ).astype(BF16)
        return carry

    loop(0, STEPS // 2, forward_second)
    each_member(lambda peer: part_copy(peer, peer).wait_recv())
    total = lax.fori_loop(
        0, group, lambda k, acc: acc + red_in[k], jnp.zeros((share, SIDE), F32)
    )
    red_out[flat] = (total * scale).astype(BF16)
    each_member(lambda peer: sum_copy(peer, flat).start())
    loop(STEPS // 2, STEPS - 1, forward_second, unroll=3)
    forward_second(STEPS - 1, 0, ahead=False)
    each_member(lambda peer: sum_copy(peer, peer).wait_recv())

    halves = [
        jnp.concatenate(
            [red_out[half * pieces + k].astype(F32) for k in range(pieces)], axis=0
        )
        for half in range(2)
    ]
    turned = halves[1][0:SIDE].T
    for a in range(3):
        rows = slice(a * CH, (a + 1) * CH)
        gsecond_ref[3 * a] = halves[0][rows, 0:CH]
        gsecond_ref[3 * a + 1] = halves[0][rows, CH : 2 * CH]
        gsecond_ref[3 * a + 2] = halves[1][rows, 0:CH]
        for b in range(3):
            lane = 64 + a * 16 + b * 4
            gfirst_ref[3 * a + b] = turned[lane : lane + CIN, 0:CH]

    for part in (px, rim, inp, hid):
        finish(*part)
    each_member(lambda peer: part_copy(peer, flat).wait_send())
    each_member(lambda peer: sum_copy(peer, flat).wait_send())


def deliver(*refs):
    sem = refs[-1]
    copies = []
    for src, dst in zip(refs[:4], refs[4:8]):
        parts = [()]
        if src.shape[-1] == PIX:
            parts = [(0, slice(None), pl.ds(k * STEP, STEP)) for k in range(STEPS)]
        for at in parts:
            a, b = (src.at[at], dst.at[at]) if at else (src, dst)
            copies.append(pltpu.make_async_copy(a, b, sem.at[len(copies)]))
    for copy in copies:
        copy.start()
    for copy in copies:
        copy.wait()


def body(cycle_maps, send_pick, recv_pick, neighbour, facing, conv_first, conv_second, cotangent):
    tile_count = lax.axis_size("tile")
    chan_count = lax.axis_size("chan")
    sub_count = lax.axis_size("sub")
    group = tile_count * chan_count * sub_count
    cap = send_pick.shape[0] // tile_count
    scale = 1.0 / math.sqrt(group * PIX)
    per_block = cap // SLOT_DEPTH
    block_rows = -(-CIN * per_block // 16) * 16
    share = 8 * -(-2 * 3 * CH // (8 * group))
    vmem = pl.BlockSpec(memory_space=pltpu.VMEM)
    smem = pl.BlockSpec(memory_space=pltpu.SMEM)
    dma = pltpu.SemaphoreType.DMA
    hbm = pl.BlockSpec(memory_space=pl.ANY)
    shapes = (
        jax.ShapeDtypeStruct((1, CH, PIX), BF16),
        jax.ShapeDtypeStruct((1, CH, PIX), BF16),
        jax.ShapeDtypeStruct((9, CIN, CH), F32),
        jax.ShapeDtypeStruct((9, CH, CH), F32),
    )
    results = pl.pallas_call(
        functools.partial(kernel, tile_count, chan_count, sub_count, cap, scale),
        out_shape=shapes,
        in_specs=[vmem, vmem, vmem, smem, smem, vmem, vmem, pl.BlockSpec(memory_space=pltpu.HBM)],
        out_specs=(vmem,) * 4,
        scratch_shapes=[
            pltpu.VMEM((CH, 48), BF16),
            pltpu.VMEM((3 * CH, 3 * CH), BF16),
            pltpu.VMEM((3 * CH, 3 * CH), BF16),
            pltpu.VMEM((2 * SIDE, 2 * SIDE), F32),
            pltpu.VMEM((CIN * PIX // SEND_DEPTH, SEND_DEPTH), F32),
            pltpu.VMEM((CIN * PIX // SEND_DEPTH, SEND_DEPTH), BF16),
            pltpu.VMEM((CH, PIX), BF16),
            pltpu.VMEM((3 * CH, (SIDE + 4) * SIDE), BF16),
            pltpu.VMEM((3 * CH, (SIDE + 2) * SIDE), BF16),
            pltpu.VMEM((16, (SIDE + 2) * SIDE), BF16),
            pltpu.VMEM((8, PIX), F32),
            pltpu.VMEM((CH, PIX), F32),
            pltpu.VMEM((CH, PIX), F32),
            pltpu.VMEM((3 * CH, 2 * SIDE), F32),
            pltpu.VMEM((tile_count, block_rows, SLOT_DEPTH), F32),
            pltpu.VMEM((tile_count, block_rows, SLOT_DEPTH), BF16),
            pltpu.VMEM((tile_count, block_rows, SLOT_DEPTH), BF16),
            pltpu.VMEM((tile_count, 4, 16, SIDE), BF16),
            pltpu.VMEM((tile_count, 4, CH, SIDE), BF16),
            pltpu.VMEM((tile_count, 4, CH, SIDE), BF16),
            pltpu.VMEM((group, share, SIDE), F32),
            pltpu.VMEM((group, share, SIDE), F32),
            pltpu.VMEM((group, share, SIDE), BF16),
        ]
        + [dma((tile_count,))] * 8
        + [dma((group,))] * 4
        + [dma(())],
        compiler_params=pltpu.CompilerParams(
            collective_id=0, has_side_effects=True, vmem_limit_bytes=VMEM_BYTES
        ),
        cost_estimate=pl.CostEstimate(
            flops=6_000_000_000, bytes_accessed=8_000_000, transcendentals=1_000_000
        ),
    )(
        cycle_maps,
        send_pick.reshape(1, -1),
        recv_pick.reshape(1, -1),
        neighbour,
        facing,
        conv_first.transpose(0, 2, 1),
        conv_second,
        cotangent,
    )
    out, ghid, gfirst, gsecond = pl.pallas_call(
        deliver,
        out_shape=shapes,
        in_specs=[vmem] * 4,
        out_specs=(hbm,) * 4,
        scratch_shapes=[dma((2 * STEPS + 2,))],
        compiler_params=pltpu.CompilerParams(vmem_limit_bytes=VMEM_BYTES),
    )(*results)
    return out, ghid, gfirst.transpose(0, 2, 1), gsecond


def solution(mesh):
    in_specs = (
        P(("groups", "chan", "sub"), None, "tile"),
        P("tile"),
        P("tile"),
        P(),
        P(),
        P(),
        P(),
        P(("groups", "chan", "sub"), None, "tile"),
    )
    out_specs = (
        P(("groups", "chan", "sub"), None, "tile"),
        P(("groups", "chan", "sub"), None, "tile"),
        P("groups", None, None),
        P("groups", None, None),
    )
    return jax.shard_map(body, mesh=mesh, in_specs=in_specs, out_specs=out_specs, check_vma=False)
```

```python
import functools
import math

import jax
import jax.numpy as jnp
from jax import lax
from jax.experimental import pallas as pl
from jax.experimental.pallas import tpu as pltpu
from jax.sharding import PartitionSpec as P

SIDE = 128
CH = 64
CIN = 3
PIX = SIDE * SIDE
ROWS = 16
STEP = ROWS * SIDE
STEPS = SIDE // ROWS
SEND_DEPTH = 256
SLOT_DEPTH = 384
MESH = pl.DeviceIdType.MESH
F32 = jnp.float32
BF16 = jnp.bfloat16
NT = (((1,), (1,)), ((), ()))
TN = (((0,), (0,)), ((), ()))


def dot(a, b):
    return jnp.dot(a, b, preferred_element_type=F32)


def dot_nt(a, b):
    return lax.dot_general(a, b, NT, preferred_element_type=F32)


def dot_tn(a, b):
    return lax.dot_general(a, b, TN, preferred_element_type=F32)


def lane_is(x, lane):
    kind = jnp.int16 if x.dtype == BF16 else jnp.int32
    return lax.broadcasted_iota(kind, (x.shape[0], SIDE), 1) == lane


def tile_rows(x):
    return [x[:, r * SIDE : (r + 1) * SIDE] for r in range(x.shape[1] // SIDE)]


def turn(x, amount):
    return x if isinstance(amount, int) and amount % SIDE == 0 else pltpu.roll(x, amount, 1)


def west_edge(rows, fill):
    return [
        jnp.where(lane_is(row, 0), jnp.zeros_like(row) if fill is None else turn(fill, (SIDE - r) % SIDE), row)
        for r, row in enumerate(rows)
    ]


def east_edge(rows, fill):
    return [
        jnp.where(lane_is(row, SIDE - 1), jnp.zeros_like(row) if fill is None else turn(fill, SIDE - 1 - r), row)
        for r, row in enumerate(rows)
    ]


def from_left(x, fill=None):
    rows = [pltpu.roll(row, 1, 1) for row in tile_rows(x)]
    return jnp.concatenate(west_edge(rows, fill), axis=1).astype(x.dtype)


def from_right(x, fill=None):
    rows = [pltpu.roll(row, SIDE - 1, 1) for row in tile_rows(x)]
    return jnp.concatenate(east_edge(rows, fill), axis=1).astype(x.dtype)


def unwind(strip, step):
    return pltpu.roll(strip, (SIDE - ROWS * step) % SIDE, 1)


def pick_edges(x, step):
    first = jnp.zeros((x.shape[0], SIDE), x.dtype)
    last = first
    for r, row in enumerate(tile_rows(x)):
        here = lane_is(row, r)
        first = jnp.where(here, turn(row, r), first)
        last = jnp.where(here, turn(row, r + 1), last)
    return pltpu.roll(first, ROWS * step, 1), pltpu.roll(last, ROWS * step, 1)


def add_edges(total, x, step):
    first, last = pick_edges(x, step)
    return total[0] + first, total[1] + last


def loop(low, high, act, carry=0, unroll=4):
    def several(k, carry):
        for u in range(unroll):
            carry = act(low + k * unroll + u, carry)
        return carry

    return lax.fori_loop(0, (high - low) // unroll, several, carry)


def one_hot(depth, index):
    shape = (depth, index.shape[1])
    position = lax.broadcasted_iota(jnp.int16, shape, 0)
    hit = position == index.astype(jnp.int16)
    return jnp.where(hit, jnp.ones(shape, BF16), jnp.zeros(shape, BF16))


def kernel(
    tile_count,
    chan_count,
    sub_count,
    cap,
    scale,
    cycle_ref,
    send_ref,
    recv_ref,
    nbr_ref,
    face_ref,
    first_ref,
    second_ref,
    cot_hbm,
    out_ref,
    ghid_ref,
    gfirst_ref,
    gsecond_ref,
    w_first_ref,
    w_fwd_ref,
    w_bwd_ref,
    weights,
    table_wide,
    table_ref,
    cot_ref,
    out_vmem,
    ghid_vmem,
    cc,
    hh,
    xx,
    tiles,
    slope,
    hgrad,
    grads,
    slots,
    block_out,
    block_in,
    strip_in,
    strip_hid,
    strip_rim,
    red_src,
    red_in,
    red_out,
    px_send,
    px_recv,
    in_send,
    in_recv,
    hid_send,
    hid_recv,
    rim_send,
    rim_recv,
    part_send,
    part_recv,
    sum_send,
    sum_recv,
    cot_sem,
    out_sem,
    ghid_sem,
):
    me = lax.axis_index("tile")
    group = tile_count * chan_count * sub_count
    flat = (me * chan_count + lax.axis_index("chan")) * sub_count + lax.axis_index("sub")
    groups_per_block = cap // SLOT_DEPTH
    block_rows = block_out.shape[1]

    def member(index):
        return {
            "tile": index // (chan_count * sub_count),
            "chan": (index // sub_count) % chan_count,
            "sub": index % sub_count,
        }

    barrier = pltpu.get_barrier_semaphore()

    def greet(k, carry):
        pl.semaphore_signal(
            barrier, inc=1, device_id=member((flat + k) % group), device_id_type=MESH
        )
        return carry

    lax.fori_loop(1, group, greet, 0)
    cot_copy = pltpu.make_async_copy(cot_hbm.at[0], cot_ref, cot_sem)
    cot_copy.start()

    for g in range(PIX // SEND_DEPTH):
        piece = cycle_ref[0, :, g * SEND_DEPTH : (g + 1) * SEND_DEPTH].astype(F32)
        for c in range(CIN):
            row = c * (PIX // SEND_DEPTH) + g
            table_wide[row : row + 1, :] = piece[c : c + 1]
    table_ref[...] = table_wide[...].astype(BF16)

    def tile_copy(src, dst, send_sem, recv_sem, peer, place):
        return pltpu.make_async_remote_copy(
            src_ref=src,
            dst_ref=dst.at[place],
            send_sem=send_sem.at[peer],
            recv_sem=recv_sem.at[place],
            device_id={"tile": peer},
            device_id_type=MESH,
        )

    def post(source, dst, send_sem, recv_sem):
        def go(k, carry):
            peer = (me + k) % tile_count
            tile_copy(source(peer), dst, send_sem, recv_sem, peer, me).start()
            return carry

        lax.fori_loop(1, tile_count, go, 0)

    def collect(source, dst, send_sem, recv_sem):
        def go(k, carry):
            peer = (me + k) % tile_count
            tile_copy(source(peer), dst, send_sem, recv_sem, peer, peer).wait_recv()
            return carry

        lax.fori_loop(1, tile_count, go, 0)

    def finish(source, dst, send_sem, recv_sem):
        def go(k, carry):
            peer = (me + k) % tile_count
            tile_copy(source(peer), dst, send_sem, recv_sem, peer, me).wait_send()
            return carry

        lax.fori_loop(1, tile_count, go, 0)

    px = (lambda peer: block_out.at[peer], block_in, px_send, px_recv)
    inp = (lambda peer: strip_in.at[me], strip_in, in_send, in_recv)
    hid = (lambda peer: strip_hid.at[me], strip_hid, hid_send, hid_recv)
    rim = (lambda peer: strip_rim.at[me], strip_rim, rim_send, rim_recv)

    flip = jnp.where(
        lax.broadcasted_iota(jnp.int32, (SIDE, SIDE), 0)
        + lax.broadcasted_iota(jnp.int32, (SIDE, SIDE), 1)
        == SIDE - 1,
        1.0,
        0.0,
    ).astype(BF16)

    def reverse(strip):
        return dot(strip.astype(BF16), flip)

    def cells(step, extra=0, rows=ROWS):
        return pl.ds(pl.multiple_of(step * STEP + extra * SIDE, SIDE), rows * SIDE)

    if block_rows != CIN * groups_per_block:
        slots[...] = jnp.zeros_like(slots)
    quads = groups_per_block // 4
    width = 4 * SLOT_DEPTH
    table_groups = PIX // SEND_DEPTH

    def fill(dest, quad):
        at = (dest * quads + quad) * width
        pick = send_ref[0:1, pl.ds(pl.multiple_of(at, SIDE), width)]
        hot = one_hot(SEND_DEPTH, pick & (SEND_DEPTH - 1))
        found = dot(table_ref[...], hot)
        mask = lax.broadcasted_iota(jnp.int32, (table_groups, width), 0) == pick // SEND_DEPTH
        for c in range(CIN):
            part = found[c * table_groups : (c + 1) * table_groups]
            value = jnp.sum(jnp.where(mask, part, 0.0), axis=0, keepdims=True)
            for q in range(4):
                row = c * groups_per_block + quad * 4 + q
                slots[dest, row : row + 1, :] = value[:, q * SLOT_DEPTH : (q + 1) * SLOT_DEPTH]

    def fill_block(dest):
        for quad in range(quads):
            fill(dest, quad)
        block_out[dest] = slots[dest].astype(BF16)

    def send_block(k, carry):
        dest = (me + k) % tile_count
        fill_block(dest)
        tile_copy(px[0](dest), *px[1:], dest, me).start()
        return carry

    pl.semaphore_wait(barrier, group - 1)
    lax.fori_loop(1, tile_count, send_block, 0)
    fill_block(me)
    block_in[me] = block_out[me]

    for a in range(3):
        for b in range(3):
            weights[a * CH : (a + 1) * CH, b * CH : (b + 1) * CH] = second_ref[
                3 * a + b
            ].astype(F32)
    w_fwd_ref[...] = weights[0 : 3 * CH, 0 : 3 * CH].astype(BF16)
    weights[...] = jnp.zeros_like(weights)
    for a in range(3):
        for b in range(3):
            weights[b * CH : (b + 1) * CH, a * CH : (a + 1) * CH] = second_ref[
                3 * a + b
            ].astype(F32)
    w_bwd_ref[...] = weights[...].T[0 : 3 * CH, 0 : 3 * CH].astype(BF16)
    weights[0:SIDE, 0:SIDE] = jnp.zeros((SIDE, SIDE), F32)
    for a in range(3):
        for b in range(3):
            at = a * 16 + b * 4
            weights[at : at + CIN, 0:CH] = first_ref[3 * a + b].astype(F32)
    w_first_ref[...] = weights[0:SIDE, 0:SIDE].T[0:CH, 0:48].astype(BF16)
    cc[:, 0 : 2 * SIDE] = jnp.zeros((3 * CH, 2 * SIDE), BF16)
    cc[:, (SIDE + 2) * SIDE : (SIDE + 4) * SIDE] = jnp.zeros((3 * CH, 2 * SIDE), BF16)

    cot_copy.wait()

    def shift_cotangent(step, columns):
        narrow = cot_ref[:, cells(step)]
        at = cells(step, 2)
        cc[0:CH, at] = from_right(narrow)
        cc[CH : 2 * CH, at] = narrow
        cc[2 * CH : 3 * CH, at] = from_left(narrow)
        return add_edges(columns, narrow, step)

    none = jnp.zeros((CH, SIDE), BF16)
    cot_columns = loop(0, STEPS, shift_cotangent, (none, none))

    def interior(step, carry):
        term = dot(w_bwd_ref[...], cc[:, cells(step, 1, ROWS + 2)])
        hgrad[:, cells(step)] = (
            term[0:CH, 2 * SIDE :]
            + term[CH : 2 * CH, SIDE : SIDE + STEP]
            + term[2 * CH :, 0:STEP]
        )
        return carry

    loop(0, STEPS // 2, interior)

    collect(*px)
    chunk = 1024

    def place(it, carry):
        at = pl.ds(pl.multiple_of(it * chunk, chunk), chunk)
        pick = recv_ref[0:1, at]
        key = ((pick // SIDE) * 171) // 512
        hot = one_hot(SLOT_DEPTH, pick - key * SLOT_DEPTH)
        table = block_in[...].reshape(tile_count * block_rows, SLOT_DEPTH)
        found = dot(table, hot)
        total = [jnp.zeros((groups_per_block, chunk), F32)] * CIN
        local = lax.broadcasted_iota(jnp.int32, (groups_per_block, chunk), 0)
        for owner in range(tile_count):
            mask = local + owner * groups_per_block == key
            for c in range(CIN):
                start = owner * block_rows + c * groups_per_block
                part = found[start : start + groups_per_block]
                total[c] = total[c] + jnp.where(mask, part, 0.0)
        row = lax.broadcasted_iota(jnp.int32, (8, chunk), 0)
        value = jnp.zeros((8, chunk), F32)
        for c in range(CIN):
            value = jnp.where(row == c, jnp.sum(total[c], axis=0, keepdims=True), value)
        tiles[:, at] = value
        return carry

    loop(0, PIX // chunk, place)

    def tall(x):
        return jnp.concatenate([x, jnp.zeros_like(x)], axis=0)

    def tile_columns(step, total):
        return add_edges(total, tiles[:, cells(step)], step)

    blank = jnp.zeros((8, SIDE), F32)
    columns = loop(0, STEPS, tile_columns, (blank, blank))
    strip_in[me, 0] = tall(tiles[:, 0:SIDE]).astype(BF16)
    strip_in[me, 1] = tall(columns[1]).astype(BF16)
    strip_in[me, 2] = reverse(tall(tiles[:, PIX - SIDE : PIX])).astype(BF16)
    strip_in[me, 3] = reverse(tall(columns[0])).astype(BF16)
    post(*inp)

    def along(column):
        return jnp.concatenate([from_right(column), column, from_left(column)], axis=0)

    def outer(b):
        return jnp.concatenate([second_ref[3 * a + b] for a in range(3)], axis=0)

    strip_rim[me, 0] = dot(w_bwd_ref[0:CH, :], cc[:, 2 * SIDE : 3 * SIDE]).astype(BF16)
    strip_rim[me, 1] = dot_tn(outer(2), along(cot_columns[1])).astype(BF16)
    south = dot(w_bwd_ref[2 * CH :, :], cc[:, (SIDE + 1) * SIDE : (SIDE + 2) * SIDE])
    strip_rim[me, 2] = reverse(south).astype(BF16)
    strip_rim[me, 3] = reverse(dot_tn(outer(0), along(cot_columns[0]))).astype(BF16)
    post(*rim)

    loop(STEPS // 2, STEPS, interior)

    def incoming(buffer):
        strips = []
        for k in range(4):
            near = nbr_ref[me, k]
            there = jnp.where(near >= 0, 1.0, 0.0)
            strip = buffer[jnp.maximum(near, 0), face_ref[me, k]].astype(F32) * there
            strips.append(reverse(strip) if k < 2 else strip)
        return strips

    collect(*inp)
    north, right, bottom, left = incoming(strip_in)

    def three(mid, first, last):
        a = from_left(mid, first)
        b = from_right(mid, last)
        return jnp.concatenate([a + pltpu.roll(mid, 4, 0), b], axis=0).astype(BF16)

    xx[:, 0:SIDE] = three(north[0:8], None, None)
    xx[:, (SIDE + 1) * SIDE :] = three(bottom[0:8], None, None)
    left, right = left[0:8], right[0:8]

    def input_copies(step, carry):
        xx[:, cells(step, 1)] = three(
            tiles[:, cells(step)], unwind(left, step), unwind(right, step)
        )
        return carry

    loop(0, STEPS, input_copies)

    def input_stack(step):
        part = xx[:, cells(step, 0, ROWS + 2)]
        return [part[:, a * SIDE : a * SIDE + STEP] for a in range(3)]

    def forward_first(step, columns):
        pre = dot(w_first_ref[...], jnp.concatenate(input_stack(step), axis=0))
        sigma = jax.nn.sigmoid(pre)
        value = pre * sigma
        slope[:, cells(step)] = sigma * (1.0 + pre * (1.0 - sigma))
        narrow = value.astype(BF16)
        at = cells(step, 1)
        hh[0:CH, at] = from_left(narrow)
        hh[CH : 2 * CH, at] = narrow
        hh[2 * CH : 3 * CH, at] = from_right(narrow)
        return add_edges(columns, narrow, step)

    columns = loop(0, STEPS, forward_first, (none, none))
    strip_hid[me, 0] = hh[CH : 2 * CH, SIDE : 2 * SIDE]
    strip_hid[me, 1] = columns[1]
    strip_hid[me, 2] = reverse(hh[CH : 2 * CH, PIX : PIX + SIDE]).astype(BF16)
    strip_hid[me, 3] = reverse(columns[0]).astype(BF16)
    post(*hid)

    collect(*rim)
    north, right, bottom, left = incoming(strip_rim)
    hgrad[:, 0:SIDE] = hgrad[:, 0:SIDE] + north
    hgrad[:, PIX - SIDE : PIX] = hgrad[:, PIX - SIDE : PIX] + bottom
    rim_west, rim_east = left, right
    grads[...] = jnp.zeros_like(grads)

    def ghid_copy(step):
        at = cells(step)
        return pltpu.make_async_copy(ghid_vmem.at[:, at], ghid_ref.at[0, :, at], ghid_sem.at[step])

    def out_copy(step):
        at = cells(step)
        return pltpu.make_async_copy(out_vmem.at[:, at], out_ref.at[0, :, at], out_sem.at[step])

    def backward_first(step, carry):
        rows = tile_rows(hgrad[:, cells(step)])
        first, last = unwind(rim_west, step), unwind(rim_east, step)
        empty = [jnp.zeros((CH, SIDE), F32)] * ROWS
        edges = east_edge(west_edge(empty, first), last)
        total = jnp.concatenate([row + edge for row, edge in zip(rows, edges)], axis=1)
        ghid_vmem[:, cells(step)] = total.astype(BF16)
        ghid_copy(step).start()
        pre_grad = (total * slope[:, cells(step)]).astype(BF16)
        stack = jnp.concatenate(
            [jnp.zeros((64, STEP), BF16)] + input_stack(step) + [jnp.zeros((16, STEP), BF16)],
            axis=0,
        )
        grads[0:CH, SIDE : 2 * SIDE] = grads[0:CH, SIDE : 2 * SIDE] + dot_nt(pre_grad, stack)
        return carry

    def backward_second(step, carry):
        part = cc[CH : 2 * CH, cells(step, 1, ROWS + 2)]
        rows = jnp.concatenate(
            [part[:, 2 * SIDE :], part[:, SIDE : SIDE + STEP], part[:, 0:STEP]], axis=0
        )
        grads[:, 0 : 3 * CH] = grads[:, 0 : 3 * CH] + dot_nt(rows, hh[:, cells(step, 1)])
        return carry

    loop(0, STEPS, lambda step, carry: backward_second(step, backward_first(step, carry)))
    collect(*hid)
    north, right, bottom, left = incoming(strip_hid)

    def halo_row(strip):
        return jnp.concatenate([from_left(strip), strip, from_right(strip)], axis=0).astype(BF16)

    hh[:, 0:SIDE] = halo_row(north)
    hh[:, (SIDE + 1) * SIDE :] = halo_row(bottom)
    left = left.astype(BF16)
    right = right.astype(BF16)
    rest = jnp.zeros((CH, SIDE), BF16)
    grads[:, 0 : 3 * CH] = grads[:, 0 : 3 * CH] + dot_nt(
        along(cot_columns[0]), jnp.concatenate([left, rest, rest], axis=0)
    ) + dot_nt(along(cot_columns[1]), jnp.concatenate([rest, rest, right], axis=0))
    grads[0:CH, 0 : 3 * CH] = grads[0:CH, 0 : 3 * CH] + dot_nt(
        cc[CH : 2 * CH, 2 * SIDE : 3 * SIDE], hh[:, 0:SIDE]
    )
    grads[2 * CH :, 0 : 3 * CH] = grads[2 * CH :, 0 : 3 * CH] + dot_nt(
        cc[CH : 2 * CH, (SIDE + 1) * SIDE : (SIDE + 2) * SIDE], hh[:, (SIDE + 1) * SIDE :]
    )

    share = red_src.shape[1]
    pieces = 3 * CH // share
    for half in range(2):
        for k in range(pieces):
            red_src[half * pieces + k] = grads[
                k * share : (k + 1) * share, half * SIDE : (half + 1) * SIDE
            ]
    for k in range(2 * pieces, group):
        red_src[k] = jnp.zeros((share, SIDE), F32)

    def part_copy(peer, place):
        return pltpu.make_async_remote_copy(
            src_ref=red_src.at[peer],
            dst_ref=red_in.at[place],
            send_sem=part_send.at[peer],
            recv_sem=part_recv.at[place],
            device_id=member(peer),
            device_id_type=MESH,
        )

    def sum_copy(peer, place):
        return pltpu.make_async_remote_copy(
            src_ref=red_out.at[place],
            dst_ref=red_out.at[place],
            send_sem=sum_send.at[peer],
            recv_sem=sum_recv.at[place],
            device_id=member(peer),
            device_id_type=MESH,
        )

    def each_member(act):
        def go(k, carry):
            act((flat + k) % group)
            return carry

        lax.fori_loop(1, group, go, 0)

    red_in[flat] = red_src[flat]
    each_member(lambda peer: part_copy(peer, flat).start())

    def hidden_halo(step, carry):
        at = cells(step, 1)
        first = west_edge(tile_rows(hh[0:CH, at]), unwind(left, step))
        last = east_edge(tile_rows(hh[2 * CH :, at]), unwind(right, step))
        hh[0:CH, at] = jnp.concatenate(first, axis=1)
        hh[2 * CH :, at] = jnp.concatenate(last, axis=1)
        return carry

    hidden_halo(0, 0)

    def forward_second(step, carry, ahead=True):
        if ahead:
            hidden_halo(step + 1, 0)
        term = dot(w_fwd_ref[...], hh[:, cells(step, 0, ROWS + 2)])
        out_vmem[:, cells(step)] = (
            term[0:CH, 0:STEP]
            + term[CH : 2 * CH, SIDE : SIDE + STEP]
            + term[2 * CH :, 2 * SIDE :]
        ).astype(BF16)
        out_copy(step).start()
        return carry

    loop(0, STEPS // 2, forward_second)
    each_member(lambda peer: part_copy(peer, peer).wait_recv())
    total = lax.fori_loop(
        0, group, lambda k, acc: acc + red_in[k], jnp.zeros((share, SIDE), F32)
    )
    red_out[flat] = (total * scale).astype(BF16)
    each_member(lambda peer: sum_copy(peer, flat).start())
    loop(STEPS // 2, STEPS - 1, forward_second, unroll=3)
    forward_second(STEPS - 1, 0, ahead=False)
    each_member(lambda peer: sum_copy(peer, peer).wait_recv())

    halves = [
        jnp.concatenate(
            [red_out[half * pieces + k].astype(F32) for k in range(pieces)], axis=0
        )
        for half in range(2)
    ]
    turned = halves[1][0:SIDE].T
    for a in range(3):
        rows = slice(a * CH, (a + 1) * CH)
        gsecond_ref[3 * a] = halves[0][rows, 0:CH]
        gsecond_ref[3 * a + 1] = halves[0][rows, CH : 2 * CH]
        gsecond_ref[3 * a + 2] = halves[1][rows, 0:CH]
        for b in range(3):
            lane = 64 + a * 16 + b * 4
            gfirst_ref[3 * a + b] = turned[lane : lane + CIN, 0:CH]

    for part in (px, rim, inp, hid):
        finish(*part)
    each_member(lambda peer: part_copy(peer, flat).wait_send())
    each_member(lambda peer: sum_copy(peer, flat).wait_send())

    def written(step, carry):
        ghid_copy(step).wait()
        out_copy(step).wait()
        return carry

    lax.fori_loop(0, STEPS, written, 0)


def deliver(*refs):
    count = (len(refs) - 2) // 3
    read_sem, write_sem = refs[3 * count :]
    reads, writes = [], []
    for src, dst, hold in zip(refs[:count], refs[count : 2 * count], refs[2 * count : 3 * count]):
        parts = [()]
        if src.shape[-1] == PIX:
            parts = [(0, slice(None), pl.ds(k * STEP, STEP)) for k in range(STEPS)]
        for at in parts:
            a, b, c = (src.at[at], hold.at[at], dst.at[at]) if at else (src, hold, dst)
            reads.append(pltpu.make_async_copy(a, b, read_sem.at[len(reads)]))
            writes.append(pltpu.make_async_copy(b, c, write_sem.at[len(writes)]))
    for copy in reads:
        copy.start()
    for read, write in zip(reads, writes):
        read.wait()
        write.start()
    for copy in writes:
        copy.wait()


def body(cycle_maps, send_pick, recv_pick, neighbour, facing, conv_first, conv_second, cotangent):
    tile_count = lax.axis_size("tile")
    chan_count = lax.axis_size("chan")
    sub_count = lax.axis_size("sub")
    group = tile_count * chan_count * sub_count
    cap = send_pick.shape[0] // tile_count
    scale = 1.0 / math.sqrt(group * PIX)
    per_block = cap // SLOT_DEPTH
    block_rows = -(-CIN * per_block // 16) * 16
    share = 8 * -(-2 * 3 * CH // (8 * group))
    vmem = pl.BlockSpec(memory_space=pltpu.VMEM)
    smem = pl.BlockSpec(memory_space=pltpu.SMEM)
    dma = pltpu.SemaphoreType.DMA
    hbm = pl.BlockSpec(memory_space=pl.ANY)
    shapes = (
        jax.ShapeDtypeStruct((1, CH, PIX), BF16),
        jax.ShapeDtypeStruct((1, CH, PIX), BF16),
        jax.ShapeDtypeStruct((9, CIN, CH), F32),
        jax.ShapeDtypeStruct((9, CH, CH), F32),
    )
    results = pl.pallas_call(
        functools.partial(kernel, tile_count, chan_count, sub_count, cap, scale),
        out_shape=shapes,
        in_specs=[vmem, vmem, vmem, smem, smem, vmem, vmem, hbm],
        out_specs=(hbm, hbm, vmem, vmem),
        scratch_shapes=[
            pltpu.VMEM((CH, 48), BF16),
            pltpu.VMEM((3 * CH, 3 * CH), BF16),
            pltpu.VMEM((3 * CH, 3 * CH), BF16),
            pltpu.VMEM((2 * SIDE, 2 * SIDE), F32),
            pltpu.VMEM((CIN * PIX // SEND_DEPTH, SEND_DEPTH), F32),
            pltpu.VMEM((CIN * PIX // SEND_DEPTH, SEND_DEPTH), BF16),
            pltpu.VMEM((CH, PIX), BF16),
            pltpu.VMEM((CH, PIX), BF16),
            pltpu.VMEM((CH, PIX), BF16),
            pltpu.VMEM((3 * CH, (SIDE + 4) * SIDE), BF16),
            pltpu.VMEM((3 * CH, (SIDE + 2) * SIDE), BF16),
            pltpu.VMEM((16, (SIDE + 2) * SIDE), BF16),
            pltpu.VMEM((8, PIX), F32),
            pltpu.VMEM((CH, PIX), F32),
            pltpu.VMEM((CH, PIX), F32),
            pltpu.VMEM((3 * CH, 2 * SIDE), F32),
            pltpu.VMEM((tile_count, block_rows, SLOT_DEPTH), F32),
            pltpu.VMEM((tile_count, block_rows, SLOT_DEPTH), BF16),
            pltpu.VMEM((tile_count, block_rows, SLOT_DEPTH), BF16),
            pltpu.VMEM((tile_count, 4, 16, SIDE), BF16),
            pltpu.VMEM((tile_count, 4, CH, SIDE), BF16),
            pltpu.VMEM((tile_count, 4, CH, SIDE), BF16),
            pltpu.VMEM((group, share, SIDE), F32),
            pltpu.VMEM((group, share, SIDE), F32),
            pltpu.VMEM((group, share, SIDE), BF16),
        ]
        + [dma((tile_count,))] * 8
        + [dma((group,))] * 4
        + [dma(()), dma((STEPS,)), dma((STEPS,))],
        compiler_params=pltpu.CompilerParams(
            collective_id=0, has_side_effects=True, vmem_limit_bytes=56 * 1024 * 1024
        ),
        cost_estimate=pl.CostEstimate(
            flops=6_000_000_000, bytes_accessed=8_000_000, transcendentals=1_000_000
        ),
    )(
        cycle_maps,
        send_pick.reshape(1, -1),
        recv_pick.reshape(1, -1),
        neighbour,
        facing,
        conv_first.transpose(0, 2, 1),
        conv_second,
        cotangent,
    )
    out, ghid, gfirst, gsecond = pl.pallas_call(
        deliver,
        out_shape=shapes,
        in_specs=[hbm] * 4,
        out_specs=(hbm,) * 4,
        scratch_shapes=[pltpu.VMEM(shape.shape, shape.dtype) for shape in shapes]
        + [dma((2 * STEPS + 2,))] * 2,
        compiler_params=pltpu.CompilerParams(vmem_limit_bytes=56 * 1024 * 1024),
    )(*results)
    return out, ghid, gfirst.transpose(0, 2, 1), gsecond


def solution(mesh):
    in_specs = (
        P(("groups", "chan", "sub"), None, "tile"),
        P("tile"),
        P("tile"),
        P(),
        P(),
        P(),
        P(),
        P(("groups", "chan", "sub"), None, "tile"),
    )
    out_specs = (
        P(("groups", "chan", "sub"), None, "tile"),
        P(("groups", "chan", "sub"), None, "tile"),
        P("groups", None, None),
        P("groups", None, None),
    )
    return jax.shard_map(body, mesh=mesh, in_specs=in_specs, out_specs=out_specs, check_vma=False)
```
